512 devices in a mesh: gx: 32 (over y, z_lo), gy: 4 (over x), gz: 4 (over z_hi, core).
Axes of the slice: x: 4, y: 8, z: 8 (z_hi: 2, z_lo: 4; z = z_hi * 4 + z_lo), core: 2. Of those that a mesh axis runs over, the one named last changes fastest.
Arguments:
- node_feat: float32 [262144, 128], P(('gx', 'gy', 'gz')), may hold values from -6 to 6
- edge_feat: float32 [1048576, 128], P(('gx', 'gy', 'gz')), may hold values from -6 to 6
- node_cot: float32 [262144, 128], P(('gx', 'gy', 'gz')), may hold values from -6 to 6
- edge_cot: float32 [1048576, 128], P(('gx', 'gy', 'gz')), may hold values from -6 to 6
- sender: int32 [1048576], P(('gx', 'gy', 'gz')), may hold values from 0 to 1375, as said below
- receiver: int32 [1048576], P(('gx', 'gy', 'gz')), may hold values from 0 to 511, as said below
- block_count: int32 [8192], P(('gx', 'gy', 'gz')), may hold values from 0 to 128, as said below
- send_rows: int32 [96, 12, 12, 32], P('gx', 'gy', 'gz'), may hold values from 0 to 511, as said below
- edge_in_weight: float32 [384, 128], replicated, may hold values from -0.3125 to 0.3125
- edge_bias: float32 [128], replicated, may hold values from -3 to 3
- edge_out_weight: float32 [128, 128], replicated, may hold values from -0.5 to 0.5
- edge_gain: float32 [128], replicated, may hold values from 0.1 to 1.9
- node_in_weight: float32 [256, 128], replicated, may hold values from -0.375 to 0.375
- node_bias: float32 [128], replicated, may hold values from -3 to 3
- node_out_weight: float32 [128, 128], replicated, may hold values from -0.5 to 0.5
- node_gain: float32 [128], replicated, may hold values from 0.1 to 1.9
Outputs:
- node_grad: float32 [262144, 128], P(('gx', 'gy', 'gz'))
- edge_grad: float32 [1048576, 128], P(('gx', 'gy', 'gz'))
- edge_in_grad: float32 [384, 128], replicated
- edge_bias_grad: float32 [128], replicated
- edge_out_grad: float32 [128, 128], replicated
- edge_gain_grad: float32 [128], replicated
- node_in_grad: float32 [256, 128], replicated
- node_bias_grad: float32 [128], replicated
- node_out_grad: float32 [128, 128], replicated
- node_gain_grad: float32 [128], replicated
The draws below stay inside these ranges and needn't reach their ends.
Inputs may be any that keep to these rules, and one draw needn't show every extreme that they name: `sender`: A value below 512 is an owned cell; otherwise it is 512 + 32 index(d) + s with s below 32, a halo slot of direction d. It never names direction 13 nor a direction whose neighbour lies outside the device grid. `receiver`: nondecreasing over the edge rows of one device. `block_count`: the nonzero blocks of a device come first; some device has no empty block. `send_rows`: the 32 cells of one list are distinct.
All inputs are finite; a program needn't handle non-finite values.
Results may differ from the reference program's by a relative error of at most 0.000088.
Values sent between devices are 32-bit elements; how exact they have to be, the bound alone decides.
No kernel may reach another device: no remote copies, remote signals or barrier semaphores. Data moves between devices by JAX's collectives and lax.ppermute only.
A program may use at most 64 MiB of HBM per device.

```python
import math
import jax
import jax.numpy as jnp
from jax import lax

HID = 128
CELLS = 512
EDGES_DEV = 2048
BLOCKS = 16
SLOT = 32
GRID_X = 32
GRID_Y = 4
GRID_Z = 4
NODES = 262144
EDGES = 1048576
DEVICES = 512


def draw_sender(key, part):
    key = jax.random.fold_in(key, 11)
    pick_key, remote_key, place_key, home_key = jax.random.split(key, 4)
    total = DEVICES * EDGES_DEV
    device = jnp.arange(total, dtype=jnp.int32) // EDGES_DEV
    coord_x = device // (GRID_Y * GRID_Z)
    coord_y = device // GRID_Z % GRID_Y
    coord_z = device % GRID_Z
    direction = jax.random.randint(pick_key, (total,), 0, 27, dtype=jnp.int32)
    step_x = direction // 9 - 1
    step_y = direction // 3 % 3 - 1
    step_z = direction % 3 - 1
    inside = (coord_x + step_x >= 0) & (coord_x + step_x < GRID_X)
    inside = inside & (coord_y + step_y >= 0) & (coord_y + step_y < GRID_Y)
    inside = inside & (coord_z + step_z >= 0) & (coord_z + step_z < GRID_Z) & (direction != 13)
    remote = jax.random.randint(remote_key, (total,), 0, 2, dtype=jnp.int32) < 1
    position = jax.random.randint(place_key, (total,), 0, SLOT, dtype=jnp.int32)
    local_row = jax.random.randint(home_key, (total,), 0, CELLS, dtype=jnp.int32)
    halo_row = CELLS + direction * SLOT + position
    return jnp.where(remote & inside, halo_row, local_row).astype(jnp.int32)


def draw_receiver(key, part):
    key = jax.random.fold_in(key, 12)
    raw_rows = jax.random.randint(key, (DEVICES, EDGES_DEV), 0, CELLS, dtype=jnp.int32)
    return jnp.sort(raw_rows, axis=1).reshape(DEVICES * EDGES_DEV)


def draw_block_count(key, part):
    key = jax.random.fold_in(key, 13)
    live_key, fill_key, top_key, device_key = jax.random.split(key, 4)
    live = jax.random.randint(live_key, (DEVICES, 1), max(1, BLOCKS // 8), BLOCKS + 1, dtype=jnp.int32)
    device_index = jnp.arange(DEVICES, dtype=jnp.int32)[:, None]
    full_device = jax.random.randint(device_key, (), 0, DEVICES, dtype=jnp.int32)
    live = jnp.where(device_index == full_device, BLOCKS, live)
    fill = jax.random.randint(fill_key, (DEVICES, BLOCKS), 64, 129, dtype=jnp.int32)
    top_block = jax.random.randint(top_key, (), 0, BLOCKS, dtype=jnp.int32)
    block_index = jnp.arange(BLOCKS, dtype=jnp.int32)[None, :]
    fill = jnp.where((block_index == top_block) & (device_index == full_device), 128, fill)
    return jnp.where(block_index < live, fill, 0).astype(jnp.int32).reshape(DEVICES * BLOCKS)


def draw_send_rows(key, part):
    key = jax.random.fold_in(key, 14)
    list_keys = jax.random.split(key, DEVICES * 27)
    rows = jax.vmap(lambda single: jax.random.permutation(single, CELLS)[:SLOT])(list_keys).astype(jnp.int32)
    rows = rows.reshape(GRID_X, GRID_Y, GRID_Z, 3, 3, 3, SLOT).transpose(0, 3, 1, 4, 2, 5, 6)
    return rows.reshape(3 * GRID_X, 3 * GRID_Y, 3 * GRID_Z, SLOT)


def levels(own_key, shape, cuts, least, high):
    factor_of = 1.0
    for dim, shards_of in cuts:
        steps = jax.random.uniform(jax.random.fold_in(jax.random.fold_in(own_key, 6), dim), (shards_of,), jnp.float32, least / len(cuts), high / len(cuts))
        factor_of = factor_of * jnp.repeat(jnp.exp(steps), shape[dim] // shards_of).reshape((-1,) + (1,) * (len(shape) - 1 - dim))
    return factor_of


def bell_draw(own_key, extent, deviation, limit, cuts=(), kind=jnp.bfloat16):
    entries = deviation * jax.random.normal(own_key, extent, jnp.float32)
    if cuts:
        entries = entries * levels(own_key, extent, cuts, -0.22, 0.18)
    return jnp.clip(entries, -limit, limit).astype(kind)


def setup_inputs(seed: int = 0) -> dict:
    keys = jax.random.split(jax.random.key(seed), 17)
    node_feat = bell_draw(keys[0], (NODES, HID), 1.0, 6.0, ((0, 512),), jnp.float32)
    edge_feat = bell_draw(keys[1], (EDGES, HID), 1.0, 6.0, ((0, 512),), jnp.float32)
    node_cot = bell_draw(keys[2], (NODES, HID), 1.0, 6.0, ((0, 512),), jnp.float32)
    edge_cot = bell_draw(keys[3], (EDGES, HID), 1.0, 6.0, ((0, 512),), jnp.float32)
    sender = draw_sender(jax.random.fold_in(keys[16], 71), 0)
    receiver = draw_receiver(jax.random.fold_in(keys[16], 71), 0)
    block_count = draw_block_count(jax.random.fold_in(keys[16], 71), 0)
    send_rows = draw_send_rows(jax.random.fold_in(keys[16], 71), 0)
    edge_in_weight = bell_draw(keys[8], (3 * HID, HID), (3 * HID) ** -0.5, 0.3125, (), jnp.float32)
    edge_bias = bell_draw(keys[9], (HID,), 0.5, 3.0, (), jnp.float32)
    edge_out_weight = bell_draw(keys[10], (HID, HID), HID ** -0.5, 0.5, (), jnp.float32)
    edge_gain = jnp.clip(1.0 + 0.18 * jax.random.normal(keys[11], (HID,), jnp.float32), 0.1, 1.9)
    node_in_weight = bell_draw(keys[12], (2 * HID, HID), (2 * HID) ** -0.5, 0.375, (), jnp.float32)
    node_bias = bell_draw(keys[13], (HID,), 0.5, 3.0, (), jnp.float32)
    node_out_weight = bell_draw(keys[14], (HID, HID), HID ** -0.5, 0.5, (), jnp.float32)
    node_gain = jnp.clip(1.0 + 0.18 * jax.random.normal(keys[15], (HID,), jnp.float32), 0.1, 1.9)
    return {"node_feat": node_feat, "edge_feat": edge_feat, "node_cot": node_cot, "edge_cot": edge_cot, "sender": sender, "receiver": receiver, "block_count": block_count, "send_rows": send_rows, "edge_in_weight": edge_in_weight, "edge_bias": edge_bias, "edge_out_weight": edge_out_weight, "edge_gain": edge_gain, "node_in_weight": node_in_weight, "node_bias": node_bias, "node_out_weight": node_out_weight, "node_gain": node_gain}


NORM_EPS = 1e-05
HIGHEST = lax.Precision.HIGHEST

def layer_norm(values, gain):
    average = lax.optimization_barrier(jnp.mean(values, axis=-1, keepdims=True))
    centred = values - average
    spread_sq = lax.optimization_barrier(jnp.mean(centred * centred, axis=-1, keepdims=True))
    return centred * lax.rsqrt(spread_sq + NORM_EPS) * gain

def edge_section(node_table, edge_feat, sender, receiver, valid_mask, edge_in_weight, edge_bias, edge_out_weight, edge_gain):
    width = edge_feat.shape[1]
    preact = jnp.dot(edge_feat, edge_in_weight[:width], precision=HIGHEST)
    preact = preact + jnp.dot(node_table[sender], edge_in_weight[width:2 * width], precision=HIGHEST)
    preact = preact + jnp.dot(node_table[receiver], edge_in_weight[2 * width:], precision=HIGHEST)
    hidden = jax.nn.silu(preact + edge_bias)
    return layer_norm(jnp.dot(hidden, edge_out_weight, precision=HIGHEST), edge_gain) * valid_mask[:, None]

def node_section(node_feat, summed, node_in_weight, node_bias, node_out_weight, node_gain):
    width = node_feat.shape[1]
    preact = jnp.dot(node_feat, node_in_weight[:width], precision=HIGHEST) + jnp.dot(summed, node_in_weight[width:], precision=HIGHEST)
    hidden = jax.nn.silu(preact + node_bias)
    return node_feat + layer_norm(jnp.dot(hidden, node_out_weight, precision=HIGHEST), node_gain)

def from_neighbours(packets):
    grid_x, grid_y, grid_z = (packets.shape[0], packets.shape[1], packets.shape[2])
    padded = jnp.pad(packets, ((1, 1), (1, 1), (1, 1), (0, 0), (0, 0), (0, 0), (0, 0), (0, 0)))
    pieces = []
    for direction in range(27):
        step_x = direction // 9 - 1
        step_y = direction // 3 % 3 - 1
        step_z = direction % 3 - 1
        pieces.append(padded[1 + step_x:1 + step_x + grid_x, 1 + step_y:1 + step_y + grid_y, 1 + step_z:1 + step_z + grid_z, 1 - step_x, 1 - step_y, 1 - step_z])
    stacked = jnp.stack(pieces, axis=3)
    return stacked.reshape(grid_x, grid_y, grid_z, 3, 3, 3, packets.shape[6], packets.shape[7])

def device_backward(item, weights):
    node_feat, received, edge_feat, node_cot, edge_cot, sender, receiver, valid_mask = item
    edge_in_weight, edge_bias, edge_out_weight, edge_gain, node_in_weight, node_bias, node_out_weight, node_gain = weights
    num_cells = node_feat.shape[0]
    node_table = jnp.concatenate([node_feat, received], axis=0)

    def edge_part(table_in, feat_in, weight_in, bias_in, weight_out, gain_in):
        return edge_section(table_in, feat_in, sender, receiver, valid_mask, weight_in, bias_in, weight_out, gain_in)
    message, edge_pull = jax.vjp(edge_part, node_table, edge_feat, edge_in_weight, edge_bias, edge_out_weight, edge_gain)
    summed = jax.ops.segment_sum(message, receiver, num_segments=num_cells, indices_are_sorted=True)
    _, node_pull = jax.vjp(node_section, node_feat, summed, node_in_weight, node_bias, node_out_weight, node_gain)
    node_grads = node_pull(node_cot)
    edge_grads = edge_pull(edge_cot + node_grads[1][receiver])
    table_grad = edge_grads[0]
    own_grad = node_grads[0] + table_grad[:num_cells]
    grads = (edge_grads[2], edge_grads[3], edge_grads[4], edge_grads[5], node_grads[2], node_grads[3], node_grads[4], node_grads[5])
    return (own_grad, table_grad[num_cells:], edge_cot + edge_grads[1], grads)

def reference(node_feat, edge_feat, node_cot, edge_cot, sender, receiver, block_count, send_rows, edge_in_weight, edge_bias, edge_out_weight, edge_gain, node_in_weight, node_bias, node_out_weight, node_gain):
    outer_mask = (jnp.arange(27) != 13).astype(jnp.float32).reshape(3, 3, 3, 1, 1)
    node_blocks = node_feat.reshape(GRID_X, GRID_Y, GRID_Z, CELLS, HID)
    row_lists = send_rows.reshape(GRID_X, 3, GRID_Y, 3, GRID_Z, 3, SLOT).transpose(0, 2, 4, 1, 3, 5, 6)
    packets = jax.vmap(jax.vmap(jax.vmap(lambda block, rows: block[rows])))(node_blocks, row_lists) * outer_mask
    received = from_neighbours(packets)
    valid_mask = (lax.broadcasted_iota(jnp.int32, (DEVICES * BLOCKS, 128), 1) < block_count[:, None]).astype(jnp.float32)
    weights = (edge_in_weight, edge_bias, edge_out_weight, edge_gain, node_in_weight, node_bias, node_out_weight, node_gain)
    items = (node_feat.reshape(DEVICES, CELLS, HID), received.reshape(DEVICES, 27 * SLOT, HID), edge_feat.reshape(DEVICES, EDGES_DEV, HID), node_cot.reshape(DEVICES, CELLS, HID), edge_cot.reshape(DEVICES, EDGES_DEV, HID), sender.reshape(DEVICES, EDGES_DEV), receiver.reshape(DEVICES, EDGES_DEV), valid_mask.reshape(DEVICES, EDGES_DEV))
    own_grad, slot_grad, edge_grad, grads = lax.map(lambda item: device_backward(item, weights), items)
    slot_grad = slot_grad.reshape(GRID_X, GRID_Y, GRID_Z, 3, 3, 3, SLOT, HID) * outer_mask
    returned = from_neighbours(slot_grad) * outer_mask
    base_rows = jnp.arange(DEVICES, dtype=jnp.int32).reshape(GRID_X, GRID_Y, GRID_Z, 1, 1, 1, 1) * CELLS
    flat_rows = (base_rows + row_lists).reshape(-1)
    node_grad = own_grad.reshape(NODES, HID) + jax.ops.segment_sum(returned.reshape(-1, HID), flat_rows, num_segments=NODES)
    grad_scale = 1.0 / math.sqrt(DEVICES * EDGES_DEV)
    summed_grads = [lax.optimization_barrier(jnp.sum(entry, axis=0)) * grad_scale for entry in grads]
    return (node_grad, edge_grad.reshape(EDGES, HID), summed_grads[0], summed_grads[1], summed_grads[2], summed_grads[3], summed_grads[4], summed_grads[5], summed_grads[6], summed_grads[7])
```

```python
import math

import jax
import jax.numpy as jnp
from jax import lax
from jax.sharding import PartitionSpec as P

NORM_EPS = 1e-05
HIGHEST = lax.Precision.HIGHEST


AXES = ("y", "zl", "x", "zh", "c")
SPLIT = (8, 4, 4, 2, 2)
GX, GY, GZ = (("y", "zl"), ("x",), ("zh", "c"))


def exchange(value):
    for dim, axis in enumerate((GX, GY, GZ)):
        peers = lax.axis_size(axis)
        up = [(i, i + 1) for i in range(peers - 1)]
        down = [(j, i) for i, j in up]
        low, mid, high = (lax.index_in_dim(value, k, axis=dim) for k in range(3))
        before = lax.ppermute(high, axis, up)
        after = lax.ppermute(low, axis, down)
        value = jnp.concatenate([before, mid, after], axis=dim)
    return value


def sum_all(rows):
    side = lax.axis_index("c")
    halves = rows.reshape(2, 512, 128)
    keep = lax.dynamic_index_in_dim(halves, side, 0, keepdims=False)
    give = lax.dynamic_index_in_dim(halves, 1 - side, 0, keepdims=False)
    swap = [(0, 1), (1, 0)]
    part = keep + lax.ppermute(give, "c", swap)
    part = lax.all_to_all(part.reshape(16, 32, 128), ("x", "zl"), 0, 0).sum(0)
    part = lax.all_to_all(jnp.broadcast_to(part, (16, 32, 128)), ("y", "zh"), 0, 0).sum(0)
    part = lax.all_to_all(jnp.broadcast_to(part, (16, 32, 128)), ("x", "zl"), 0, 0)
    part = part.reshape(512, 128)
    other = lax.ppermute(part, "c", swap)
    low = jnp.where(side == 0, part, other)
    high = jnp.where(side == 0, other, part)
    return jnp.concatenate([low, high], axis=0)


def layer_norm(values, gain):
    average = jnp.mean(values, axis=-1, keepdims=True)
    centred = values - average
    spread_sq = jnp.mean(centred * centred, axis=-1, keepdims=True)
    return centred * lax.rsqrt(spread_sq + NORM_EPS) * gain


def edge_section(
    node_table,
    edge_feat,
    sender,
    receiver,
    valid_mask,
    edge_in_weight,
    edge_bias,
    edge_out_weight,
    edge_gain,
):
    width = edge_feat.shape[1]
    preact = jnp.dot(edge_feat, edge_in_weight[:width], precision=HIGHEST)
    preact = preact + jnp.dot(
        node_table[sender], edge_in_weight[width : 2 * width], precision=HIGHEST
    )
    preact = preact + jnp.dot(node_table[receiver], edge_in_weight[2 * width :], precision=HIGHEST)
    hidden = jax.nn.silu(preact + edge_bias)
    return (
        layer_norm(jnp.dot(hidden, edge_out_weight, precision=HIGHEST), edge_gain)
        * valid_mask[:, None]
    )


def node_section(node_feat, summed, node_in_weight, node_bias, node_out_weight, node_gain):
    width = node_feat.shape[1]
    preact = jnp.dot(node_feat, node_in_weight[:width], precision=HIGHEST) + jnp.dot(
        summed, node_in_weight[width:], precision=HIGHEST
    )
    hidden = jax.nn.silu(preact + node_bias)
    return node_feat + layer_norm(jnp.dot(hidden, node_out_weight, precision=HIGHEST), node_gain)


def outer_directions():
    index = lax.broadcasted_iota(jnp.int32, (27,), 0)
    return (index != 13).astype(jnp.float32).reshape(3, 3, 3, 1, 1)


def on_device(
    node_feat,
    edge_feat,
    node_cot,
    edge_cot,
    sender,
    receiver,
    block_count,
    send_rows,
    edge_in_weight,
    edge_bias,
    edge_out_weight,
    edge_gain,
    node_in_weight,
    node_bias,
    node_out_weight,
    node_gain,
):
    num_cells, width = node_feat.shape
    edge_rows = edge_feat.shape[0]
    slot_count = send_rows.shape[3]
    total_rows = lax.axis_size(AXES) * edge_rows
    grad_scale = 1.0 / math.sqrt(total_rows)
    outer_mask = outer_directions()
    packets = node_feat[send_rows] * outer_mask
    received = exchange(packets)
    node_table = jnp.concatenate([node_feat, received.reshape(27 * slot_count, width)], axis=0)
    valid_mask = (
        (lax.broadcasted_iota(jnp.int32, (block_count.shape[0], 128), 1) < block_count[:, None])
        .astype(jnp.float32)
        .reshape(edge_rows)
    )

    def edge_part(table_in, feat_in, weight_in, bias_in, weight_out, gain_in):
        return edge_section(
            table_in, feat_in, sender, receiver, valid_mask, weight_in, bias_in, weight_out, gain_in
        )

    message, edge_pull = jax.vjp(
        edge_part, node_table, edge_feat, edge_in_weight, edge_bias, edge_out_weight, edge_gain
    )
    summed = jax.ops.segment_sum(message, receiver, num_segments=num_cells, indices_are_sorted=True)
    _, node_pull = jax.vjp(
        node_section, node_feat, summed, node_in_weight, node_bias, node_out_weight, node_gain
    )
    node_grads = node_pull(node_cot)
    node_weights = (node_grads[2], node_grads[3], node_grads[4], node_grads[5])
    edge_grads = edge_pull(edge_cot + node_grads[1][receiver])
    parts = (edge_grads[2], edge_grads[3], edge_grads[4], edge_grads[5]) + node_weights
    rows = jnp.concatenate([part.reshape(-1, 128) for part in parts])
    rows = sum_all(jnp.pad(rows, ((0, 1024 - rows.shape[0]), (0, 0))))
    combined, start = [], 0
    for part in parts:
        size = part.size // 128
        combined.append(rows[start : start + size].reshape(part.shape))
        start += size
    edge_weights = combined[:4]
    node_weights = combined[4:]
    table_grad = edge_grads[0]
    slot_grads = table_grad[num_cells:].reshape(3, 3, 3, slot_count, width) * outer_mask
    returned = exchange(slot_grads) * outer_mask
    halo_sum = jax.ops.segment_sum(
        returned.reshape(27 * slot_count, width),
        send_rows.reshape(27 * slot_count),
        num_segments=num_cells,
    )
    node_grad = node_grads[0] + table_grad[:num_cells] + halo_sum
    edge_grad = edge_cot + edge_grads[1]
    return (
        node_grad,
        edge_grad,
        edge_weights[0] * grad_scale,
        edge_weights[1] * grad_scale,
        edge_weights[2] * grad_scale,
        edge_weights[3] * grad_scale,
        node_weights[0] * grad_scale,
        node_weights[1] * grad_scale,
        node_weights[2] * grad_scale,
        node_weights[3] * grad_scale,
    )


def solution(mesh):
    fine = jax.sharding.Mesh(mesh.devices.reshape(SPLIT), AXES)
    return jax.shard_map(
        on_device,
        mesh=fine,
        in_specs=(
            P(AXES, None),
            P(AXES, None),
            P(AXES, None),
            P(AXES, None),
            P(AXES),
            P(AXES),
            P(AXES),
            P(GX, GY, GZ, None),
            P(),
            P(),
            P(),
            P(),
            P(),
            P(),
            P(),
            P(),
        ),
        out_specs=(
            P(AXES, None),
            P(AXES, None),
            P(),
            P(),
            P(),
            P(),
            P(),
            P(),
            P(),
            P(),
        ),
        check_vma=False,
    )
```

```python
import functools
import math

import jax
import jax.numpy as jnp
from jax import lax
from jax.experimental import pallas as pl
from jax.experimental.pallas import tpu as pltpu
from jax.sharding import PartitionSpec as P

NORM_EPS = 1e-05
AXES = ("y", "zl", "x", "zh", "c")
SPLIT = (8, 4, 4, 2, 2)
GX, GY, GZ = (("y", "zl"), ("x",), ("zh", "c"))
HID, CELLS, EDGES, SLOT = 128, 512, 2048, 32
SLAB = 9 * SLOT
HALO = 896
BLOCK = 512
F32, BF16 = jnp.float32, jnp.bfloat16
VMEM = pl.BlockSpec(memory_space=pltpu.VMEM)
SMEM = pl.BlockSpec(memory_space=pltpu.SMEM)


def split(value):
    high = value.astype(BF16)
    low = (value - high.astype(F32)).astype(BF16)
    return jnp.concatenate([high, low], axis=1)


def fold(value):
    return value[:, :HID] + value[:, HID:]


def mix(weight):
    high = weight.astype(BF16)
    low = (weight - high.astype(F32)).astype(BF16)
    top = jnp.concatenate([high, low], axis=1)
    bottom = jnp.concatenate([high, jnp.zeros_like(low)], axis=1)
    return jnp.concatenate([top, bottom], axis=0)


def mul(left, right):
    return jnp.dot(left, right, preferred_element_type=F32)


def mul_rows(left, right):
    return lax.dot_general(left, right, (((0,), (0,)), ((), ())), preferred_element_type=F32)


def quad(value):
    top, bottom = value[:HID], value[HID:]
    return fold(top) + fold(bottom)


def centred(weight):
    return weight - jnp.mean(weight, axis=1, keepdims=True)


def silu_parts(preact):
    gate = 1.0 / (1.0 + jnp.exp(-preact))
    hidden = preact * gate
    return hidden, gate + hidden * (1.0 - gate)


def spread_columns(index, out_ref):
    turned = jnp.transpose(index.astype(F32)).astype(jnp.int32)
    for block in range(EDGES // HID):
        column = turned[:, block : block + 1]
        out_ref[block * HID : (block + 1) * HID, :] = jnp.broadcast_to(column, (HID, HID))


def hot_rows(column, width, base=0):
    lane = lax.broadcasted_iota(jnp.int32, column.shape, 1)
    parts = [
        (column == lane + (base + start)).astype(F32).astype(BF16) for start in range(0, width, HID)
    ]
    return jnp.concatenate(parts, axis=1)


def hot_columns(ref, first, height, base=0):
    level = lax.broadcasted_iota(jnp.int32, (height, HID), 0) + base
    parts = []
    for j in range(BLOCK // HID):
        row = ref[pl.ds(first + j, 1), :]
        parts.append((level == row).astype(F32).astype(BF16))
    return jnp.concatenate(parts, axis=1)


def list_rows(lists_ref):
    turned = jnp.transpose(lists_ref[...].astype(F32)).astype(jnp.int32)
    cell = lax.broadcasted_iota(jnp.int32, (SLOT, CELLS), 1)
    parts = []
    for d in range(27):
        hot = (turned[:SLOT, d : d + 1] == cell).astype(F32)
        parts.append((hot if d != 13 else hot * 0.0).astype(BF16))
    return jnp.concatenate(parts, axis=0)


def packet_kernel(node_ref, lists_ref, low_ref, mid_ref, high_ref):
    rows = fold(mul(list_rows(lists_ref), split(node_ref[...])))
    low_ref[...] = rows[:SLAB]
    mid_ref[...] = rows[SLAB : 2 * SLAB]
    high_ref[...] = rows[2 * SLAB :]


def before_kernel(
    node_ref, edge_ref, sender_ref, receiver_ref, weight_ref, bias_ref, out_ref, send_ref, recv_ref
):
    spread_columns(sender_ref[...], send_ref)
    spread_columns(receiver_ref[...], recv_ref)
    own = split(node_ref[...])
    sent = fold(mul(own, mix(weight_ref[HID : 2 * HID, :])))
    got = fold(mul(own, mix(weight_ref[2 * HID :, :])))
    table = jnp.concatenate([split(sent), split(got)], axis=0)
    first = mix(weight_ref[:HID, :])
    bias = bias_ref[...]

    def step(i, carry):
        rows = pl.ds(pl.multiple_of(i * BLOCK, BLOCK), BLOCK)
        hot = jnp.concatenate(
            [hot_rows(send_ref[rows, :], CELLS), hot_rows(recv_ref[rows, :], CELLS)], axis=1
        )
        value = mul(hot, table) + mul(split(edge_ref[rows, :]), first)
        out_ref[rows, :] = fold(value) + bias
        return carry

    lax.fori_loop(0, EDGES // BLOCK, step, 0)


def main_kernel(
    count_ref,
    side_ref,
    pre_ref,
    halo0_ref,
    halo1_ref,
    halo2_ref,
    edge_ref,
    cot_ref,
    sender_ref,
    receiver_ref,
    node_ref,
    node_cot_ref,
    ein_ref,
    eout_ref,
    egain_ref,
    nin_ref,
    nbias_ref,
    nout_ref,
    ngain_ref,
    keep_ref,
    give_ref,
    back0_ref,
    back1_ref,
    back2_ref,
    own_ref,
    got_ref,
    base_ref,
    dpre_ref,
    send_ref,
    recv_ref,
    order_ref,
    hid_ref,
    slope_ref,
    norm_ref,
    inv_ref,
    sum_ref,
    table_ref,
    grads_ref,
    acc_ref,
    row_ref,
    turn_ref,
):
    raw = sender_ref[...]
    slot = raw - CELLS
    direction = slot >> 5
    third = (direction * 43) >> 7
    moved = CELLS + SLAB * (direction - 3 * third) + SLOT * third + (slot & (SLOT - 1))
    order_ref[...] = jnp.where(raw < CELLS, raw, moved)
    spread_columns(order_ref[...], send_ref)
    spread_columns(receiver_ref[...], recv_ref)
    halo = jnp.concatenate([halo0_ref[...], halo1_ref[...], halo2_ref[...]], axis=0)
    halo = jnp.concatenate([halo, jnp.zeros((HALO - 3 * SLAB, HID), F32)], axis=0)
    halo_split = split(halo)
    table_ref[...] = split(fold(mul(halo_split, mix(ein_ref[HID : 2 * HID, :]))))
    out_weight = centred(eout_ref[...])
    out_mix = mix(out_weight)
    turn_ref[...] = mix(jnp.transpose(out_weight))
    gain = egain_ref[...]
    sum_ref[...] = jnp.zeros_like(sum_ref)

    def live(i):
        row = lax.broadcasted_iota(jnp.int32, (HID, HID), 0)
        blocks = BLOCK // HID
        return jnp.concatenate([row < count_ref[i * blocks + j] for j in range(blocks)], axis=0)

    def forward(i, carry):
        rows = pl.ds(pl.multiple_of(i * BLOCK, BLOCK), BLOCK)
        hot = hot_rows(send_ref[rows, :], HALO, CELLS)
        preact = pre_ref[rows, :] + fold(mul(hot, table_ref[...]))
        hidden, slope = silu_parts(preact)
        hidden = split(hidden)
        hid_ref[rows, :] = hidden
        slope_ref[rows, :] = slope
        value = fold(mul(hidden, out_mix))
        inv = lax.rsqrt(jnp.mean(value * value, axis=1, keepdims=True) + NORM_EPS)
        norm = value * inv
        norm_ref[rows, :] = norm
        inv_ref[rows, :] = jnp.broadcast_to(inv, norm.shape)
        message = jnp.where(live(i), norm * gain, 0.0)
        first = i * (BLOCK // HID)
        sum_ref[...] += mul(hot_columns(receiver_ref, first, CELLS), split(message))
        return carry

    lax.fori_loop(0, EDGES // BLOCK, forward, 0)

    node_split = split(node_ref[...])

    @pl.when(count_ref[0] >= 0)
    def _():
        summed = split(fold(sum_ref[...]))
        preact = fold(mul(node_split, mix(nin_ref[:HID, :]))) + fold(mul(summed, mix(nin_ref[HID:, :])))
        hidden, slope = silu_parts(preact + nbias_ref[...])
        hidden = split(hidden)
        node_weight = centred(nout_ref[...])
        value = fold(mul(hidden, mix(node_weight)))
        inv = lax.rsqrt(jnp.mean(value * value, axis=1, keepdims=True) + NORM_EPS)
        norm = value * inv
        cot = node_cot_ref[...]
        dnorm = cot * ngain_ref[...]
        dvalue = split(inv * (dnorm - norm * jnp.mean(dnorm * norm, axis=1, keepdims=True)))
        dpre = fold(mul(dvalue, mix(jnp.transpose(node_weight)))) * slope
        dpre_split = split(dpre)
        grads_ref[1, 0:HID, :] = quad(mul_rows(node_split, dpre_split))
        grads_ref[1, HID : 2 * HID, :] = quad(mul_rows(summed, dpre_split))
        grads_ref[1, 2 * HID : 3 * HID, :] = centred(quad(mul_rows(hidden, dvalue)))
        grads_ref[1, 3 * HID :, :] = jnp.zeros((HID, HID), F32)
        grads_ref[1, 3 * HID + 2 : 3 * HID + 3, :] = jnp.sum(dpre, axis=0, keepdims=True)
        grads_ref[1, 3 * HID + 3 : 3 * HID + 4, :] = jnp.sum(cot * norm, axis=0, keepdims=True)
        base_ref[...] = cot + fold(mul(dpre_split, mix(jnp.transpose(nin_ref[:HID, :]))))
        table_ref[:CELLS, :] = split(fold(mul(dpre_split, mix(jnp.transpose(nin_ref[HID:, :])))))

    sum_ref[...] = jnp.zeros_like(sum_ref)
    row_ref[...] = jnp.zeros_like(row_ref)
    acc_ref[...] = jnp.zeros_like(acc_ref)

    def backward(i, carry):
        rows = pl.ds(pl.multiple_of(i * BLOCK, BLOCK), BLOCK)
        grad = cot_ref[rows, :] + fold(mul(hot_rows(recv_ref[rows, :], CELLS), table_ref[:CELLS, :]))
        grad = jnp.where(live(i), grad, 0.0)
        norm = norm_ref[rows, :]
        dnorm = grad * gain
        dvalue = inv_ref[rows, :] * (dnorm - norm * jnp.mean(dnorm * norm, axis=1, keepdims=True))
        dvalue = split(dvalue)
        dpre = fold(mul(dvalue, turn_ref[...])) * slope_ref[rows, :]
        dpre_ref[rows, :] = dpre
        dpre_split = split(dpre)
        acc_ref[0] += mul_rows(hid_ref[rows, :], dvalue)
        acc_ref[1] += mul_rows(split(edge_ref[rows, :]), dpre_split)
        first = i * (BLOCK // HID)
        sum_ref[...] += mul(hot_columns(receiver_ref, first, CELLS), dpre_split)
        row_ref[...] += mul(hot_columns(order_ref, first, CELLS + HALO), dpre_split)
        bias_grad, gain_grad = carry
        return (
            bias_grad + jnp.sum(dpre, axis=0, keepdims=True),
            gain_grad + jnp.sum(grad * norm, axis=0, keepdims=True),
        )

    zero = jnp.zeros((1, HID), F32)
    bias_grad, gain_grad = lax.fori_loop(0, EDGES // BLOCK, backward, (zero, zero))
    own = fold(row_ref[:CELLS, :])
    back = fold(row_ref[CELLS:, :])
    got = fold(sum_ref[...])
    own_ref[...] = own
    got_ref[...] = got
    back0_ref[...] = back[:SLAB]
    back1_ref[...] = back[SLAB : 2 * SLAB]
    back2_ref[...] = back[2 * SLAB : 3 * SLAB]
    grads_ref[0, 0:HID, :] = quad(acc_ref[1])
    grads_ref[0, HID : 2 * HID, :] = quad(mul_rows(node_split, split(own))) + quad(mul_rows(halo_split, split(back)))
    grads_ref[0, 2 * HID : 3 * HID, :] = quad(mul_rows(node_split, split(got)))
    grads_ref[0, 3 * HID :, :] = centred(quad(acc_ref[0]))
    grads_ref[1, 3 * HID : 3 * HID + 1, :] = bias_grad
    grads_ref[1, 3 * HID + 1 : 3 * HID + 2, :] = gain_grad
    side = side_ref[0]
    keep_ref[...] = grads_ref[side]
    give_ref[...] = grads_ref[1 - side]


def edge_kernel(cot_ref, dpre_ref, base_ref, own_ref, got_ref, weight_ref, edge_ref, part_ref):
    first = mix(jnp.transpose(weight_ref[:HID, :]))

    def step(i, carry):
        rows = pl.ds(pl.multiple_of(i * BLOCK, BLOCK), BLOCK)
        edge_ref[rows, :] = cot_ref[rows, :] + fold(mul(split(dpre_ref[rows, :]), first))
        return carry

    lax.fori_loop(0, EDGES // BLOCK, step, 0)
    second = mix(jnp.transpose(weight_ref[HID : 2 * HID, :]))
    third = mix(jnp.transpose(weight_ref[2 * HID :, :]))
    value = mul(split(own_ref[...]), second) + mul(split(got_ref[...]), third)
    part_ref[...] = base_ref[...] + fold(value)


def node_kernel(lists_ref, low_ref, mid_ref, high_ref, part_ref, weight_ref, out_ref):
    back = jnp.concatenate([low_ref[...], mid_ref[...], high_ref[...]], axis=0)
    summed = fold(mul_rows(list_rows(lists_ref), split(back)))
    turned = mix(jnp.transpose(weight_ref[HID : 2 * HID, :]))
    out_ref[...] = part_ref[...] + fold(mul(split(summed), turned))


def finish_kernel(
    side_ref, part_ref, other_ref, ein_ref, eout_ref, nin_ref, nout_ref, eb, eg, nb, ng, *, scale
):
    mine = side_ref[0] == 0
    part, other = part_ref[...] * scale, other_ref[...] * scale
    low = jnp.where(mine, part, other)
    high = jnp.where(mine, other, part)
    ein_ref[...] = low[: 3 * HID]
    eout_ref[...] = low[3 * HID :]
    nin_ref[...] = high[: 2 * HID]
    nout_ref[...] = high[2 * HID : 3 * HID]
    for k, ref in enumerate((eb, eg, nb, ng)):
        ref[...] = high[3 * HID + k : 3 * HID + k + 1]


def call(body, outs, ins, scratch=(), smem=(), flops=0):
    shapes = [jax.ShapeDtypeStruct(shape, F32) for shape in outs]
    size = 4 * sum(math.prod(shape) for shape in outs) + sum(4 * v.size for v in ins)
    return pl.pallas_call(
        body,
        out_shape=shapes,
        in_specs=[SMEM] * len(smem) + [VMEM] * len(ins),
        out_specs=[VMEM] * len(outs),
        scratch_shapes=[pltpu.VMEM(shape, kind) for shape, kind in scratch],
        cost_estimate=pl.CostEstimate(flops=flops, bytes_accessed=size, transcendentals=0),
        compiler_params=pltpu.CompilerParams(vmem_limit_bytes=40 * 1024 * 1024),
    )(*smem, *ins)


def make_packets(node_feat, lists):
    return call(packet_kernel, [(SLAB, HID)] * 3, [node_feat, lists], flops=10**9)


def edge_before(node_feat, edge_feat, sender, receiver, weight, bias):
    return call(
        before_kernel,
        [(EDGES, HID)],
        [node_feat, edge_feat, sender, receiver, weight, bias],
        scratch=[((EDGES, HID), jnp.int32)] * 2,
        flops=3 * 10**9,
    )[0]


def main_step(count, side, operands):
    return call(
        main_kernel,
        [(CELLS, HID)] * 2 + [(SLAB, HID)] * 3 + [(CELLS, HID)] * 3 + [(EDGES, HID)],
        operands,
        scratch=[
            ((EDGES, HID), jnp.int32),
            ((EDGES, HID), jnp.int32),
            ((EDGES // HID, HID), jnp.int32),
            ((EDGES, 2 * HID), BF16),
            ((EDGES, HID), F32),
            ((EDGES, HID), F32),
            ((EDGES, HID), F32),
            ((CELLS, 2 * HID), F32),
            ((HALO, 2 * HID), BF16),
            ((2, CELLS, HID), F32),
            ((2, 2 * HID, 2 * HID), F32),
            ((CELLS + HALO, 2 * HID), F32),
            ((2 * HID, 2 * HID), BF16),
        ],
        smem=[count, side],
        flops=10**10,
    )


def edge_after(cot, dpre, base, own, got, weight):
    return call(
        edge_kernel,
        [(EDGES, HID), (CELLS, HID)],
        [cot, dpre, base, own, got, weight],
        flops=10**9,
    )


def node_after(lists, back, part, weight):
    return call(node_kernel, [(CELLS, HID)], [lists, *back, part, weight], flops=10**9)[0]


def finish(side, part, other, scale):
    shapes = [(3 * HID, HID), (HID, HID), (2 * HID, HID), (HID, HID)] + [(1, HID)] * 4
    return call(
        functools.partial(finish_kernel, scale=scale), shapes, [part, other], smem=[side], flops=10**6
    )


def from_both(low, high, axis):
    peers = lax.axis_size(axis)
    up = [(i, i + 1) for i in range(peers - 1)]
    down = [(j, i) for i, j in up]
    return lax.ppermute(high, axis, up), lax.ppermute(low, axis, down)


def exchange_out(low, mid, high):
    before, after = from_both(low, high, GX)
    pieces = [piece.reshape(3, 3, SLOT, HID) for piece in (before, mid, after)]
    low, mid, high = (jnp.stack([piece[k] for piece in pieces]) for k in range(3))
    before, after = from_both(low, high, GY)
    pieces = (before, mid, after)
    low, mid, high = (jnp.stack([piece[:, k] for piece in pieces], axis=1) for k in range(3))
    before, after = from_both(low, high, GZ)
    return [piece.reshape(SLAB, HID) for piece in (before, mid, after)]


def exchange_back(low, mid, high):
    before, after = from_both(low, high, GZ)
    pieces = [piece.reshape(3, 3, SLOT, HID) for piece in (before, mid, after)]
    low, mid, high = (jnp.stack([piece[:, k] for piece in pieces], axis=1) for k in range(3))
    before, after = from_both(low, high, GY)
    pieces = (before, mid, after)
    low, mid, high = (jnp.stack([piece[k] for piece in pieces], axis=0) for k in range(3))
    before, after = from_both(low, high, GX)
    return [piece.reshape(SLAB, HID) for piece in (before, mid, after)]


def sum_half(keep, give):
    swap = [(0, 1), (1, 0)]
    part = keep + lax.ppermute(give, "c", swap)
    part = lax.all_to_all(part.reshape(16, 32, HID), ("x", "zl"), 0, 0).sum(0)
    part = lax.all_to_all(jnp.broadcast_to(part, (16, 32, HID)), ("y", "zh"), 0, 0).sum(0)
    part = lax.all_to_all(jnp.broadcast_to(part, (16, 32, HID)), ("x", "zl"), 0, 0)
    part = part.reshape(CELLS, HID)
    return part, lax.ppermute(part, "c", swap)


def on_device(
    node_feat,
    edge_feat,
    node_cot,
    edge_cot,
    sender,
    receiver,
    block_count,
    send_rows,
    edge_in_weight,
    edge_bias,
    edge_out_weight,
    edge_gain,
    node_in_weight,
    node_bias,
    node_out_weight,
    node_gain,
):
    scale = 1.0 / math.sqrt(lax.axis_size(AXES) * EDGES)
    side = lax.axis_index("c").astype(jnp.int32).reshape(1)
    lists = jnp.pad(send_rows.reshape(27, SLOT), ((0, 5), (0, HID - SLOT)))
    sender = sender.reshape(EDGES // HID, HID)
    receiver = receiver.reshape(EDGES // HID, HID)
    edge_bias, edge_gain, node_bias, node_gain = (
        row.reshape(1, HID) for row in (edge_bias, edge_gain, node_bias, node_gain)
    )
    halo = exchange_out(*make_packets(node_feat, lists))
    before = edge_before(node_feat, edge_feat, sender, receiver, edge_in_weight, edge_bias)
    operands = [before, *halo, edge_feat, edge_cot, sender, receiver, node_feat, node_cot]
    operands += [edge_in_weight, edge_out_weight, edge_gain]
    operands += [node_in_weight, node_bias, node_out_weight, node_gain]
    keep, give, back0, back1, back2, own, got, base, dpre = main_step(block_count, side, operands)
    part, other = sum_half(keep, give)
    edge_grad, own_part = edge_after(edge_cot, dpre, base, own, got, edge_in_weight)
    back = exchange_back(back0, back1, back2)
    node_grad = node_after(lists, back, own_part, edge_in_weight)
    ein, eout, nin, nout, eb, eg, nb, ng = finish(side, part, other, scale)
    vectors = [row.reshape(HID) for row in (eb, eg, nb, ng)]
    return (
        node_grad,
        edge_grad,
        ein,
        vectors[0],
        eout,
        vectors[1],
        nin,
        vectors[2],
        nout,
        vectors[3],
    )


def solution(mesh):
    fine = jax.sharding.Mesh(mesh.devices.reshape(SPLIT), AXES)
    return jax.shard_map(
        on_device,
        mesh=fine,
        in_specs=(
            P(AXES, None),
            P(AXES, None),
            P(AXES, None),
            P(AXES, None),
            P(AXES),
            P(AXES),
            P(AXES),
            P(GX, GY, GZ, None),
            P(),
            P(),
            P(),
            P(),
            P(),
            P(),
            P(),
            P(),
        ),
        out_specs=(
            P(AXES, None),
            P(AXES, None),
            P(),
            P(),
            P(),
            P(),
            P(),
            P(),
            P(),
            P(),
        ),
        check_vma=False,
    )
```

```python
import functools
import math

import jax
import jax.numpy as jnp
from jax import lax
from jax.experimental import pallas as pl
from jax.experimental.pallas import tpu as pltpu
from jax.sharding import PartitionSpec as P

NORM_EPS = 1e-05
AXES = ("y", "zl", "x", "zh", "c")
SPLIT = (8, 4, 4, 2, 2)
GX, GY, GZ = (("y", "zl"), ("x",), ("zh", "c"))
SWAP = [(0, 1), (1, 0)]
HID, CELLS, EDGES, SLOT = 128, 512, 2048, 32
SLAB = 9 * SLOT
HALO = 896
BLOCK = 512
F32, BF16 = jnp.float32, jnp.bfloat16
VMEM = pl.BlockSpec(memory_space=pltpu.VMEM)
SMEM = pl.BlockSpec(memory_space=pltpu.SMEM)


def split(value):
    high = value.astype(BF16)
    low = (value - high.astype(F32)).astype(BF16)
    return jnp.concatenate([high, low], axis=1)


def fold(value):
    return value[:, :HID] + value[:, HID:]


def mix(weight):
    high = weight.astype(BF16)
    low = (weight - high.astype(F32)).astype(BF16)
    top = jnp.concatenate([high, low], axis=1)
    bottom = jnp.concatenate([high, jnp.zeros_like(low)], axis=1)
    return jnp.concatenate([top, bottom], axis=0)


def mul(left, right):
    return jnp.dot(left, right, preferred_element_type=F32)


def mul_rows(left, right):
    return lax.dot_general(left, right, (((0,), (0,)), ((), ())), preferred_element_type=F32)


def quad(value):
    top, bottom = value[:HID], value[HID:]
    return fold(top) + fold(bottom)


def centred(weight):
    return weight - jnp.mean(weight, axis=1, keepdims=True)


def silu_parts(preact):
    gate = 1.0 / (1.0 + jnp.exp(-preact))
    hidden = preact * gate
    return hidden, gate + hidden * (1.0 - gate)


def spread_columns(index, out_ref):
    turned = jnp.transpose(index.astype(F32)).astype(jnp.int32)
    for block in range(EDGES // HID):
        column = turned[:, block : block + 1]
        out_ref[block * HID : (block + 1) * HID, :] = jnp.broadcast_to(column, (HID, HID))


def hot_rows(column, width, base=0):
    lane = lax.broadcasted_iota(jnp.int32, column.shape, 1)
    parts = [
        (column == lane + (base + start)).astype(F32).astype(BF16) for start in range(0, width, HID)
    ]
    return jnp.concatenate(parts, axis=1)


def hot_columns(ref, first, height, base=0):
    level = lax.broadcasted_iota(jnp.int32, (height, HID), 0) + base
    parts = []
    for j in range(BLOCK // HID):
        row = ref[pl.ds(first + j, 1), :]
        parts.append((level == row).astype(F32).astype(BF16))
    return jnp.concatenate(parts, axis=1)


def parity(dim):
    return lax.axis_index(("zl", "x", "c")[dim]) & 1


def near_first(odd, entry):
    return entry if entry == 1 else jnp.where(odd == 0, 2 - entry, entry)


def list_rows(lists_ref, index_ref):
    index_ref[...] = jnp.zeros_like(index_ref)
    for k in range(27):
        x, y, z = (
            near_first(parity(dim), entry) for dim, entry in enumerate((k // 9, k // 3 % 3, k % 3))
        )
        index_ref[k : k + 1, :SLOT] = lists_ref[x, y, pl.ds(z, 1), :]
    turned = jnp.transpose(index_ref[...].astype(F32)).astype(jnp.int32)
    cell = lax.broadcasted_iota(jnp.int32, (SLOT, CELLS), 1)
    parts = []
    for k in range(27):
        hot = (turned[:SLOT, k : k + 1] == cell).astype(F32)
        parts.append((hot if k != 13 else hot * 0.0).astype(BF16))
    return jnp.concatenate(parts, axis=0)


def packet_kernel(node_ref, lists_ref, first_ref, mid_ref, second_ref, index_ref):
    rows = fold(mul(list_rows(lists_ref, index_ref), split(node_ref[...])))
    first_ref[...] = rows[:SLAB]
    mid_ref[...] = rows[SLAB : 2 * SLAB]
    second_ref[...] = rows[2 * SLAB :]


def regroup_kernel(in0, in1, in2, out0, out1, out2, *, chunk):
    for i, source in enumerate((in0, in1, in2)):
        base = source.shape[0] - SLAB if i == 0 else 0
        for j, target in enumerate((out0, out1, out2)):
            for k in range(SLAB // (3 * chunk)):
                to = (3 * k + i) * chunk
                at = base + (3 * k + j) * chunk
                target[to : to + chunk, :] = source[at : at + chunk, :]


def before_kernel(
    node_ref,
    edge_ref,
    sender_ref,
    receiver_ref,
    ein_ref,
    ebias_ref,
    eout_ref,
    nin_ref,
    nbias_ref,
    nout_ref,
    pre_ref,
    node_pre_ref,
    send_ref,
    recv_ref,
    order_ref,
    mix_ref,
):
    raw = sender_ref[...]
    slot = raw - CELLS
    direction = slot >> 5
    third = (direction * 43) >> 7
    ninth = (third * 43) >> 7
    x, y, z = (
        2 - entry + parity(dim) * (2 * entry - 2)
        for dim, entry in enumerate((ninth, third - 3 * ninth, direction - 3 * third))
    )
    moved = CELLS + SLAB * z + SLOT * (3 * x + y) + (slot & (SLOT - 1))
    order_ref[...] = jnp.where(raw < CELLS, raw, moved)
    spread_columns(order_ref[...], send_ref)
    spread_columns(receiver_ref[...], recv_ref)
    own = split(node_ref[...])
    halo_mix = mix(ein_ref[HID : 2 * HID, :])
    sent = fold(mul(own, halo_mix))
    got = fold(mul(own, mix(ein_ref[2 * HID :, :])))
    table = jnp.concatenate([split(sent), split(got)], axis=0)
    first = mix(ein_ref[:HID, :])
    for i in range(EDGES // BLOCK):
        rows = slice(i * BLOCK, (i + 1) * BLOCK)
        hot = jnp.concatenate(
            [hot_rows(send_ref[rows, :], CELLS), hot_rows(recv_ref[rows, :], CELLS)], axis=1
        )
        value = mul(hot, table) + mul(split(edge_ref[rows, :]), first)
        pre_ref[rows, :] = fold(value) + ebias_ref[...]
    node_pre_ref[...] = fold(mul(own, mix(nin_ref[:HID, :]))) + nbias_ref[...]
    edge_out, node_out = centred(eout_ref[...]), centred(nout_ref[...])
    mix_ref[0] = halo_mix
    mix_ref[1] = mix(edge_out)
    mix_ref[2] = mix(jnp.transpose(edge_out))
    mix_ref[3] = mix(nin_ref[HID:, :])
    mix_ref[4] = mix(node_out)
    mix_ref[5] = mix(jnp.transpose(node_out))
    mix_ref[6] = mix(jnp.transpose(nin_ref[:HID, :]))
    mix_ref[7] = mix(jnp.transpose(nin_ref[HID:, :]))


def main_kernel(
    count_ref,
    halo0_ref,
    halo1_ref,
    halo2_ref,
    pre_ref,
    node_pre_ref,
    send_ref,
    recv_ref,
    order_ref,
    mix_ref,
    receiver_ref,
    node_ref,
    node_cot_ref,
    cot_ref,
    edge_ref,
    egain_ref,
    ngain_ref,
    back0_ref,
    back1_ref,
    back2_ref,
    own_ref,
    got_ref,
    base_ref,
    dpre_ref,
    acc_ref,
    rest_ref,
    hid_ref,
    slope_ref,
    norm_ref,
    inv_ref,
    sum_ref,
    table_ref,
    row_ref,
):
    halo = [halo0_ref[...], halo1_ref[...], halo2_ref[...], jnp.zeros((HALO - 3 * SLAB, HID), F32)]
    halo_split = split(jnp.concatenate(halo, axis=0))
    table_ref[...] = split(fold(mul(halo_split, mix_ref[0])))
    gain = egain_ref[...]

    def live(i):
        row = lax.broadcasted_iota(jnp.int32, (HID, HID), 0)
        blocks = BLOCK // HID
        return jnp.concatenate([row < count_ref[i * blocks + j] for j in range(blocks)], axis=0)

    for i in range(EDGES // BLOCK):
        rows = slice(i * BLOCK, (i + 1) * BLOCK)
        hot = hot_rows(send_ref[rows, :], HALO, CELLS)
        preact = pre_ref[rows, :] + fold(mul(hot, table_ref[...]))
        hidden, slope = silu_parts(preact)
        hidden = split(hidden)
        hid_ref[rows, :] = hidden
        slope_ref[rows, :] = slope
        value = fold(mul(hidden, mix_ref[1]))
        inv = lax.rsqrt(jnp.mean(value * value, axis=1, keepdims=True) + NORM_EPS)
        norm = value * inv
        norm_ref[rows, :] = norm
        inv_ref[rows, :] = jnp.broadcast_to(inv, norm.shape)
        message = jnp.where(live(i), norm * gain, 0.0)
        term = mul(hot_columns(receiver_ref, i * (BLOCK // HID), CELLS), split(message))
        sum_ref[...] = term if i == 0 else sum_ref[...] + term

    node_split = split(node_ref[...])
    summed = split(fold(sum_ref[...]))
    hidden, slope = silu_parts(node_pre_ref[...] + fold(mul(summed, mix_ref[3])))
    hidden = split(hidden)
    value = fold(mul(hidden, mix_ref[4]))
    inv = lax.rsqrt(jnp.mean(value * value, axis=1, keepdims=True) + NORM_EPS)
    norm = value * inv
    cot = node_cot_ref[...]
    dnorm = cot * ngain_ref[...]
    dvalue = split(inv * (dnorm - norm * jnp.mean(dnorm * norm, axis=1, keepdims=True)))
    dpre = fold(mul(dvalue, mix_ref[5])) * slope
    dpre_split = split(dpre)
    table_ref[:CELLS, :] = split(fold(mul(dpre_split, mix_ref[7])))
    base_ref[...] = cot + fold(mul(dpre_split, mix_ref[6]))
    rest_ref[0:HID, :] = quad(mul_rows(node_split, dpre_split))
    rest_ref[HID : 2 * HID, :] = quad(mul_rows(summed, dpre_split))
    rest_ref[2 * HID : 3 * HID, :] = centred(quad(mul_rows(hidden, dvalue)))
    rest_ref[3 * HID :, :] = jnp.zeros((HID, HID), F32)
    rest_ref[3 * HID + 2 : 3 * HID + 3, :] = jnp.sum(dpre, axis=0, keepdims=True)
    rest_ref[3 * HID + 3 : 3 * HID + 4, :] = jnp.sum(cot * norm, axis=0, keepdims=True)

    bias_grad = gain_grad = jnp.zeros((1, HID), F32)
    for i in range(EDGES // BLOCK):
        rows = slice(i * BLOCK, (i + 1) * BLOCK)
        hot = hot_rows(recv_ref[rows, :], CELLS)
        grad = cot_ref[rows, :] + fold(mul(hot, table_ref[:CELLS, :]))
        grad = jnp.where(live(i), grad, 0.0)
        norm = norm_ref[rows, :]
        dnorm = grad * gain
        dvalue = inv_ref[rows, :] * (dnorm - norm * jnp.mean(dnorm * norm, axis=1, keepdims=True))
        dvalue = split(dvalue)
        dpre = fold(mul(dvalue, mix_ref[2])) * slope_ref[rows, :]
        dpre_ref[rows, :] = dpre
        dpre_split = split(dpre)
        first = i * (BLOCK // HID)
        terms = (
            mul(hot_columns(order_ref, first, CELLS + HALO), dpre_split),
            mul(hot_columns(receiver_ref, first, CELLS), dpre_split),
            mul_rows(hid_ref[rows, :], dvalue),
            mul_rows(split(edge_ref[rows, :]), dpre_split),
        )
        targets = (row_ref, sum_ref, acc_ref.at[0], acc_ref.at[1])
        for target, term in zip(targets, terms):
            target[...] = term if i == 0 else target[...] + term
        bias_grad += jnp.sum(dpre, axis=0, keepdims=True)
        gain_grad += jnp.sum(grad * norm, axis=0, keepdims=True)
    own_ref[...] = fold(row_ref[:CELLS, :])
    got_ref[...] = fold(sum_ref[...])
    for k, ref in enumerate((back0_ref, back1_ref, back2_ref)):
        start = CELLS + k * SLAB
        ref[...] = fold(row_ref[start : start + SLAB, :])
    rest_ref[3 * HID : 3 * HID + 1, :] = bias_grad
    rest_ref[3 * HID + 1 : 3 * HID + 2, :] = gain_grad


def weight_kernel(
    node_ref,
    halo0_ref,
    halo1_ref,
    halo2_ref,
    back0_ref,
    back1_ref,
    back2_ref,
    own_ref,
    got_ref,
    acc_ref,
    rest_ref,
    keep_ref,
    give_ref,
    grads_ref,
):
    node_split = split(node_ref[...])
    sent = quad(mul_rows(node_split, split(own_ref[...])))
    for halo, back in ((halo0_ref, back0_ref), (halo1_ref, back1_ref), (halo2_ref, back2_ref)):
        sent += quad(mul_rows(split(halo[...]), split(back[...])))
    grads_ref[0, 0:HID, :] = quad(acc_ref[1])
    grads_ref[0, HID : 2 * HID, :] = sent
    grads_ref[0, 2 * HID : 3 * HID, :] = quad(mul_rows(node_split, split(got_ref[...])))
    grads_ref[0, 3 * HID :, :] = centred(quad(acc_ref[0]))
    grads_ref[1] = rest_ref[...]
    side = parity(2)
    keep_ref[...] = grads_ref[side]
    give_ref[:CELLS, :] = grads_ref[1 - side]
    give_ref[CELLS:, :] = back0_ref[...]


def spread_kernel(terms_ref, out_ref):
    total = terms_ref[0]
    for k in range(1, terms_ref.shape[0]):
        total += terms_ref[k]
    for k in range(out_ref.shape[0]):
        out_ref[k] = total


def add_kernel(keep_ref, taken_ref, out_ref):
    out_ref[...] = keep_ref[...] + taken_ref[:CELLS, :]


def edge_kernel(cot_ref, dpre_ref, base_ref, own_ref, got_ref, weight_ref, edge_ref, part_ref):
    first = mix(jnp.transpose(weight_ref[:HID, :]))

    def step(i, carry):
        rows = pl.ds(pl.multiple_of(i * BLOCK, BLOCK), BLOCK)
        edge_ref[rows, :] = cot_ref[rows, :] + fold(mul(split(dpre_ref[rows, :]), first))
        return carry

    lax.fori_loop(0, EDGES // BLOCK, step, 0)
    second = mix(jnp.transpose(weight_ref[HID : 2 * HID, :]))
    third = mix(jnp.transpose(weight_ref[2 * HID :, :]))
    value = mul(split(own_ref[...]), second) + mul(split(got_ref[...]), third)
    part_ref[...] = base_ref[...] + fold(value)


def node_kernel(
    lists_ref, first_ref, mid_ref, second_ref, part_ref, weight_ref, out_ref, index_ref
):
    back = jnp.concatenate([first_ref[...], mid_ref[...], second_ref[...]], axis=0)
    summed = fold(mul_rows(list_rows(lists_ref, index_ref), split(back)))
    turned = mix(jnp.transpose(weight_ref[HID : 2 * HID, :]))
    out_ref[...] = part_ref[...] + fold(mul(split(summed), turned))


def finish_kernel(
    part_ref, other_ref, ein_ref, eout_ref, nin_ref, nout_ref, eb, eg, nb, ng, *, scale
):
    mine = parity(2) == 0
    part, other = part_ref[...] * scale, other_ref[...] * scale
    low = jnp.where(mine, part, other)
    high = jnp.where(mine, other, part)
    ein_ref[...] = low[: 3 * HID]
    eout_ref[...] = low[3 * HID :]
    nin_ref[...] = high[: 2 * HID]
    nout_ref[...] = high[2 * HID : 3 * HID]
    for k, ref in enumerate((eb, eg, nb, ng)):
        ref[...] = high[3 * HID + k : 3 * HID + k + 1]


def call(body, outs, ins, scratch=(), smem=(), flops=0, limit=12):
    outs = [out if isinstance(out[0], tuple) else (out, F32) for out in outs]
    shapes = [jax.ShapeDtypeStruct(shape, kind) for shape, kind in outs]
    size = 4 * sum(math.prod(shape) for shape, _ in outs) + sum(4 * v.size for v in ins)
    return pl.pallas_call(
        body,
        out_shape=shapes,
        in_specs=[SMEM] * len(smem) + [VMEM] * len(ins),
        out_specs=[VMEM] * len(outs),
        scratch_shapes=[pltpu.VMEM(shape, kind) for shape, kind in scratch],
        cost_estimate=pl.CostEstimate(flops=flops, bytes_accessed=size, transcendentals=0),
        compiler_params=pltpu.CompilerParams(vmem_limit_bytes=limit * 1024 * 1024),
    )(*smem, *ins)


def make_packets(node_feat, lists):
    return call(
        packet_kernel,
        [(SLAB, HID)] * 3,
        [node_feat, lists],
        scratch=[((SLOT, HID), jnp.int32)],
        flops=10**9,
    )


def regroup(pieces, chunk):
    body = functools.partial(regroup_kernel, chunk=chunk)
    return call(body, [(SLAB, HID)] * 3, pieces)


def edge_before(*operands):
    wide = (EDGES, HID)
    return call(
        before_kernel,
        [
            wide,
            (CELLS, HID),
            (wide, jnp.int32),
            (wide, jnp.int32),
            ((EDGES // HID, HID), jnp.int32),
            ((8, 2 * HID, 2 * HID), BF16),
        ],
        operands,
        flops=3 * 10**9,
        limit=20,
    )


def main_step(count, operands):
    square = (2 * HID, 2 * HID)
    wide = (EDGES, HID)
    return call(
        main_kernel,
        [(SLAB, HID)] * 3 + [(CELLS, HID)] * 3 + [wide, (2, *square), (CELLS, HID)],
        operands,
        scratch=[
            ((EDGES, 2 * HID), BF16),
            (wide, F32),
            (wide, F32),
            (wide, F32),
            ((CELLS, 2 * HID), F32),
            ((HALO, 2 * HID), BF16),
            ((CELLS + HALO, 2 * HID), F32),
        ],
        smem=[count],
        flops=10**10,
        limit=28,
    )


def weight_step(*operands):
    return call(
        weight_kernel,
        [(CELLS, HID), (CELLS + SLAB, HID)],
        operands,
        scratch=[((2, CELLS, HID), F32)],
        flops=10**9,
    )


def edge_after(cot, dpre, base, own, got, weight):
    return call(
        edge_kernel,
        [(EDGES, HID), (CELLS, HID)],
        [cot, dpre, base, own, got, weight],
        flops=10**9,
    )


def node_after(lists, back, part, weight):
    return call(
        node_kernel,
        [(CELLS, HID)],
        [lists, *back, part, weight],
        scratch=[((SLOT, HID), jnp.int32)],
        flops=10**9,
    )[0]


def finish(part, other, scale):
    shapes = [(3 * HID, HID), (HID, HID), (2 * HID, HID), (HID, HID)] + [(1, HID)] * 4
    return call(
        functools.partial(finish_kernel, scale=scale), shapes, [part, other], flops=10**6
    )


def swaps(axis):
    peers = lax.axis_size(axis)
    pairs = [[(i, i + 1) for i in range(start, peers - 1, 2)] for start in (0, 1)]
    return [sorted(some + [(j, i) for i, j in some]) for some in pairs]


def trade(first, second, axis):
    near, far = swaps(axis)
    second = lax.ppermute(second, axis, far)
    return lax.ppermute(first, axis, near), second


def join(values):
    return lax.optimization_barrier(values)


def sum_spread(terms, copies):
    return call(spread_kernel, [(copies, *terms.shape[1:])], [terms])[0]


def scatter_half(part):
    return lax.all_to_all(part.reshape(32, 16, HID), ("x", "zl", "zh"), 0, 0)


def every_term(terms):
    return lax.all_to_all(sum_spread(terms, 8), "y", 0, 0)


def gather_half(terms):
    part = lax.all_to_all(sum_spread(terms, 32), ("x", "zl", "zh"), 0, 0)
    return part.reshape(CELLS, HID)


def on_device(
    node_feat,
    edge_feat,
    node_cot,
    edge_cot,
    sender,
    receiver,
    block_count,
    send_rows,
    edge_in_weight,
    edge_bias,
    edge_out_weight,
    edge_gain,
    node_in_weight,
    node_bias,
    node_out_weight,
    node_gain,
):
    scale = 1.0 / math.sqrt(lax.axis_size(AXES) * EDGES)
    sender = sender.reshape(EDGES // HID, HID)
    receiver = receiver.reshape(EDGES // HID, HID)
    edge_bias, edge_gain, node_bias, node_gain = (
        row.reshape(1, HID) for row in (edge_bias, edge_gain, node_bias, node_gain)
    )
    first, mid, second = make_packets(node_feat, send_rows)
    first, second = trade(first, second, GX)
    before = edge_before(
        node_feat,
        edge_feat,
        sender,
        receiver,
        edge_in_weight,
        edge_bias,
        edge_out_weight,
        node_in_weight,
        node_bias,
        node_out_weight,
    )
    first, second, before = join((first, second, before))
    first, mid, second = regroup((first, mid, second), 3 * SLOT)
    first, second = trade(first, second, GY)
    first, mid, second = regroup((first, mid, second), SLOT)
    first, second = trade(first, second, GZ)
    halo = (first, mid, second)
    rest = (receiver, node_feat, node_cot, edge_cot, edge_feat, edge_gain, node_gain)
    *back, own, got, base, dpre, square, rows = main_step(block_count, (*halo, *before, *rest))
    second = lax.ppermute(back[2], GZ, swaps(GZ)[1])
    keep, give = weight_step(node_feat, *halo, *back, own, got, square, rows)
    mid = back[1]
    taken = lax.ppermute(give, "c", SWAP)
    part = scatter_half(call(add_kernel, [(CELLS, HID)], [keep, taken])[0])
    edge_grad, own_part = edge_after(edge_cot, dpre, base, own, got, edge_in_weight)
    first, mid, second = regroup((taken, mid, second), SLOT)
    part, first, mid, second, edge_grad, own_part = join(
        (part, first, mid, second, edge_grad, own_part)
    )
    part = every_term(part)
    first, second = trade(first, second, GY)
    first, mid, second = regroup((first, mid, second), 3 * SLOT)
    part, first, mid, second = join((part, first, mid, second))
    part = gather_half(part)
    first, second = trade(first, second, GX)
    node_grad = node_after(send_rows, (first, mid, second), own_part, edge_in_weight)
    part, node_grad = join((part, node_grad))
    other = lax.ppermute(part, "c", SWAP)
    ein, eout, nin, nout, eb, eg, nb, ng = finish(part, other, scale)
    vectors = [row.reshape(HID) for row in (eb, eg, nb, ng)]
    return (
        node_grad,
        edge_grad,
        ein,
        vectors[0],
        eout,
        vectors[1],
        nin,
        vectors[2],
        nout,
        vectors[3],
    )


def solution(mesh):
    fine = jax.sharding.Mesh(mesh.devices.reshape(SPLIT), AXES)
    return jax.shard_map(
        on_device,
        mesh=fine,
        in_specs=(
            P(AXES, None),
            P(AXES, None),
            P(AXES, None),
            P(AXES, None),
            P(AXES),
            P(AXES),
            P(AXES),
            P(GX, GY, GZ, None),
            P(),
            P(),
            P(),
            P(),
            P(),
            P(),
            P(),
            P(),
        ),
        out_specs=(
            P(AXES, None),
            P(AXES, None),
            P(),
            P(),
            P(),
            P(),
            P(),
            P(),
            P(),
            P(),
        ),
        check_vma=False,
    )
```

```python
import functools
import math

import jax
import jax.numpy as jnp
from jax import lax
from jax.experimental import pallas as pl
from jax.experimental.pallas import tpu as pltpu
from jax.sharding import PartitionSpec as P

NORM_EPS = 1e-05
AXES = ("y", "zl", "x", "zh", "c")
SPLIT = (8, 4, 4, 2, 2)
GX, GY, GZ = (("y", "zl"), ("x",), ("zh", "c"))
SWAP = [(0, 1), (1, 0)]
HID, CELLS, EDGES, SLOT = 128, 512, 2048, 32
SLAB = 9 * SLOT
HALO = 896
BLOCK = 512
F32, BF16 = jnp.float32, jnp.bfloat16
VMEM = pl.BlockSpec(memory_space=pltpu.VMEM)
SMEM = pl.BlockSpec(memory_space=pltpu.SMEM)


def split(value):
    high = value.astype(BF16)
    low = (value - high.astype(F32)).astype(BF16)
    return jnp.concatenate([high, low], axis=1)


def fold(value):
    return value[:, :HID] + value[:, HID:]


def mix(weight):
    high = weight.astype(BF16)
    low = (weight - high.astype(F32)).astype(BF16)
    top = jnp.concatenate([high, low], axis=1)
    bottom = jnp.concatenate([high, jnp.zeros_like(low)], axis=1)
    return jnp.concatenate([top, bottom], axis=0)


def mul(left, right):
    return jnp.dot(left, right, preferred_element_type=F32)


def mul_rows(left, right):
    return lax.dot_general(left, right, (((0,), (0,)), ((), ())), preferred_element_type=F32)


def quad(value):
    top, bottom = value[:HID], value[HID:]
    return fold(top) + fold(bottom)


def centred(weight):
    return weight - jnp.mean(weight, axis=1, keepdims=True)


def silu_parts(preact):
    gate = 1.0 / (1.0 + jnp.exp(-preact))
    hidden = preact * gate
    return hidden, gate + hidden * (1.0 - gate)


def spread_columns(index, out_ref):
    turned = jnp.transpose(index.astype(F32)).astype(jnp.int32)
    for block in range(EDGES // HID):
        column = turned[:, block : block + 1]
        out_ref[block * HID : (block + 1) * HID, :] = jnp.broadcast_to(column, (HID, HID))


def hot_rows(column, width, base=0):
    lane = lax.broadcasted_iota(jnp.int32, column.shape, 1)
    parts = [
        (column == lane + (base + start)).astype(F32).astype(BF16) for start in range(0, width, HID)
    ]
    return jnp.concatenate(parts, axis=1)


def hot_columns(ref, first, height, base=0):
    level = lax.broadcasted_iota(jnp.int32, (height, HID), 0) + base
    parts = []
    for j in range(BLOCK // HID):
        row = ref[pl.ds(first + j, 1), :]
        parts.append((level == row).astype(F32).astype(BF16))
    return jnp.concatenate(parts, axis=1)


def parity(dim):
    return lax.axis_index(("zl", "x", "c")[dim]) & 1


def near_first(odd, entry):
    return entry if entry == 1 else jnp.where(odd == 0, 2 - entry, entry)


def list_rows(lists_ref, index_ref):
    index_ref[...] = jnp.zeros_like(index_ref)
    for k in range(27):
        x, y, z = (
            near_first(parity(dim), entry) for dim, entry in enumerate((k // 9, k // 3 % 3, k % 3))
        )
        index_ref[k : k + 1, :SLOT] = lists_ref[x, y, pl.ds(z, 1), :]
    turned = jnp.transpose(index_ref[...].astype(F32)).astype(jnp.int32)
    cell = lax.broadcasted_iota(jnp.int32, (SLOT, CELLS), 1)
    parts = []
    for k in range(27):
        hot = (turned[:SLOT, k : k + 1] == cell).astype(F32)
        parts.append((hot if k != 13 else hot * 0.0).astype(BF16))
    return jnp.concatenate(parts, axis=0)


def packet_kernel(node_ref, lists_ref, first_ref, mid_ref, second_ref, index_ref):
    rows = fold(mul(list_rows(lists_ref, index_ref), split(node_ref[...])))
    first_ref[...] = rows[:SLAB]
    mid_ref[...] = rows[SLAB : 2 * SLAB]
    second_ref[...] = rows[2 * SLAB :]


def regroup_kernel(in0, in1, in2, out0, out1, out2, *, chunk):
    for i, source in enumerate((in0, in1, in2)):
        base = source.shape[0] - SLAB if i == 0 else 0
        for j, target in enumerate((out0, out1, out2)):
            for k in range(SLAB // (3 * chunk)):
                to = (3 * k + i) * chunk
                at = base + (3 * k + j) * chunk
                target[to : to + chunk, :] = source[at : at + chunk, :]


def before_kernel(
    node_ref,
    edge_ref,
    sender_ref,
    receiver_ref,
    ein_ref,
    ebias_ref,
    eout_ref,
    nin_ref,
    nbias_ref,
    nout_ref,
    pre_ref,
    node_pre_ref,
    send_ref,
    recv_ref,
    order_ref,
    mix_ref,
):
    raw = sender_ref[...]
    slot = raw - CELLS
    direction = slot >> 5
    third = (direction * 43) >> 7
    ninth = (third * 43) >> 7
    x, y, z = (
        2 - entry + parity(dim) * (2 * entry - 2)
        for dim, entry in enumerate((ninth, third - 3 * ninth, direction - 3 * third))
    )
    moved = CELLS + SLAB * z + SLOT * (3 * x + y) + (slot & (SLOT - 1))
    order_ref[...] = jnp.where(raw < CELLS, raw, moved)
    spread_columns(order_ref[...], send_ref)
    spread_columns(receiver_ref[...], recv_ref)
    own = split(node_ref[...])
    halo_mix = mix(ein_ref[HID : 2 * HID, :])
    sent = fold(mul(own, halo_mix))
    got = fold(mul(own, mix(ein_ref[2 * HID :, :])))
    table = jnp.concatenate([split(sent), split(got)], axis=0)
    first = mix(ein_ref[:HID, :])
    for i in range(EDGES // BLOCK):
        rows = slice(i * BLOCK, (i + 1) * BLOCK)
        hot = jnp.concatenate(
            [hot_rows(send_ref[rows, :], CELLS), hot_rows(recv_ref[rows, :], CELLS)], axis=1
        )
        value = mul(hot, table) + mul(split(edge_ref[rows, :]), first)
        pre_ref[rows, :] = fold(value) + ebias_ref[...]
    node_pre_ref[...] = fold(mul(own, mix(nin_ref[:HID, :]))) + nbias_ref[...]
    edge_out, node_out = centred(eout_ref[...]), centred(nout_ref[...])
    mix_ref[0] = halo_mix
    mix_ref[1] = mix(edge_out)
    mix_ref[2] = mix(jnp.transpose(edge_out))
    mix_ref[3] = mix(nin_ref[HID:, :])
    mix_ref[4] = mix(node_out)
    mix_ref[5] = mix(jnp.transpose(node_out))
    mix_ref[6] = mix(jnp.transpose(nin_ref[:HID, :]))
    mix_ref[7] = mix(jnp.transpose(nin_ref[HID:, :]))
    mix_ref[8] = mix(jnp.transpose(ein_ref[:HID, :]))


def main_kernel(
    count_ref,
    halo0_ref,
    halo1_ref,
    halo2_ref,
    pre_ref,
    node_pre_ref,
    send_ref,
    recv_ref,
    order_ref,
    mix_ref,
    receiver_ref,
    node_ref,
    node_cot_ref,
    cot_ref,
    edge_ref,
    egain_ref,
    ngain_ref,
    back0_ref,
    back1_ref,
    back2_ref,
    own_ref,
    got_ref,
    base_ref,
    edge_grad_ref,
    acc_ref,
    rest_ref,
    hid_ref,
    slope_ref,
    norm_ref,
    inv_ref,
    sum_ref,
    table_ref,
    row_ref,
):
    halo = [halo0_ref[...], halo1_ref[...], halo2_ref[...], jnp.zeros((HALO - 3 * SLAB, HID), F32)]
    halo_split = split(jnp.concatenate(halo, axis=0))
    table_ref[...] = split(fold(mul(halo_split, mix_ref[0])))
    gain = egain_ref[...]

    def live(i):
        row = lax.broadcasted_iota(jnp.int32, (HID, HID), 0)
        blocks = BLOCK // HID
        return jnp.concatenate([row < count_ref[i * blocks + j] for j in range(blocks)], axis=0)

    for i in range(EDGES // BLOCK):
        rows = slice(i * BLOCK, (i + 1) * BLOCK)
        hot = hot_rows(send_ref[rows, :], HALO, CELLS)
        preact = pre_ref[rows, :] + fold(mul(hot, table_ref[...]))
        hidden, slope = silu_parts(preact)
        hidden = split(hidden)
        hid_ref[rows, :] = hidden
        slope_ref[rows, :] = slope
        value = fold(mul(hidden, mix_ref[1]))
        inv = lax.rsqrt(jnp.mean(value * value, axis=1, keepdims=True) + NORM_EPS)
        norm = value * inv
        norm_ref[rows, :] = norm
        inv_ref[rows, :] = jnp.broadcast_to(inv, norm.shape)
        message = jnp.where(live(i), norm * gain, 0.0)
        term = mul(hot_columns(receiver_ref, i * (BLOCK // HID), CELLS), split(message))
        sum_ref[...] = term if i == 0 else sum_ref[...] + term

    node_split = split(node_ref[...])
    summed = split(fold(sum_ref[...]))
    hidden, slope = silu_parts(node_pre_ref[...] + fold(mul(summed, mix_ref[3])))
    hidden = split(hidden)
    value = fold(mul(hidden, mix_ref[4]))
    inv = lax.rsqrt(jnp.mean(value * value, axis=1, keepdims=True) + NORM_EPS)
    norm = value * inv
    cot = node_cot_ref[...]
    dnorm = cot * ngain_ref[...]
    dvalue = split(inv * (dnorm - norm * jnp.mean(dnorm * norm, axis=1, keepdims=True)))
    dpre = fold(mul(dvalue, mix_ref[5])) * slope
    dpre_split = split(dpre)
    table_ref[:CELLS, :] = split(fold(mul(dpre_split, mix_ref[7])))
    base_ref[...] = cot + fold(mul(dpre_split, mix_ref[6]))
    rest_ref[0:HID, :] = quad(mul_rows(node_split, dpre_split))
    rest_ref[HID : 2 * HID, :] = quad(mul_rows(summed, dpre_split))
    rest_ref[2 * HID : 3 * HID, :] = centred(quad(mul_rows(hidden, dvalue)))
    rest_ref[3 * HID :, :] = jnp.zeros((HID, HID), F32)
    rest_ref[3 * HID + 2 : 3 * HID + 3, :] = jnp.sum(dpre, axis=0, keepdims=True)
    rest_ref[3 * HID + 3 : 3 * HID + 4, :] = jnp.sum(cot * norm, axis=0, keepdims=True)

    bias_grad = gain_grad = jnp.zeros((1, HID), F32)
    for i in range(EDGES // BLOCK):
        rows = slice(i * BLOCK, (i + 1) * BLOCK)
        hot = hot_rows(recv_ref[rows, :], CELLS)
        grad = cot_ref[rows, :] + fold(mul(hot, table_ref[:CELLS, :]))
        grad = jnp.where(live(i), grad, 0.0)
        norm = norm_ref[rows, :]
        dnorm = grad * gain
        dvalue = inv_ref[rows, :] * (dnorm - norm * jnp.mean(dnorm * norm, axis=1, keepdims=True))
        dvalue = split(dvalue)
        dpre = fold(mul(dvalue, mix_ref[2])) * slope_ref[rows, :]
        dpre_split = split(dpre)
        edge_grad_ref[rows, :] = cot_ref[rows, :] + fold(mul(dpre_split, mix_ref[8]))
        first = i * (BLOCK // HID)
        terms = (
            mul(hot_columns(order_ref, first, CELLS + HALO), dpre_split),
            mul(hot_columns(receiver_ref, first, CELLS), dpre_split),
            mul_rows(hid_ref[rows, :], dvalue),
            mul_rows(split(edge_ref[rows, :]), dpre_split),
        )
        targets = (row_ref, sum_ref, acc_ref.at[0], acc_ref.at[1])
        for target, term in zip(targets, terms):
            target[...] = term if i == 0 else target[...] + term
        bias_grad += jnp.sum(dpre, axis=0, keepdims=True)
        gain_grad += jnp.sum(grad * norm, axis=0, keepdims=True)
    own_ref[...] = fold(row_ref[:CELLS, :])
    got_ref[...] = fold(sum_ref[...])
    for k, ref in enumerate((back0_ref, back1_ref, back2_ref)):
        start = CELLS + k * SLAB
        ref[...] = fold(row_ref[start : start + SLAB, :])
    rest_ref[3 * HID : 3 * HID + 1, :] = bias_grad
    rest_ref[3 * HID + 1 : 3 * HID + 2, :] = gain_grad


def weight_kernel(
    node_ref,
    halo0_ref,
    halo1_ref,
    halo2_ref,
    back0_ref,
    back1_ref,
    back2_ref,
    own_ref,
    got_ref,
    acc_ref,
    rest_ref,
    keep_ref,
    give_ref,
    grads_ref,
):
    node_split = split(node_ref[...])
    sent = quad(mul_rows(node_split, split(own_ref[...])))
    for halo, back in ((halo0_ref, back0_ref), (halo1_ref, back1_ref), (halo2_ref, back2_ref)):
        sent += quad(mul_rows(split(halo[...]), split(back[...])))
    grads_ref[0, 0:HID, :] = quad(acc_ref[1])
    grads_ref[0, HID : 2 * HID, :] = sent
    grads_ref[0, 2 * HID : 3 * HID, :] = quad(mul_rows(node_split, split(got_ref[...])))
    grads_ref[0, 3 * HID :, :] = centred(quad(acc_ref[0]))
    grads_ref[1] = rest_ref[...]
    side = parity(2)
    keep_ref[...] = grads_ref[side]
    give_ref[:CELLS, :] = grads_ref[1 - side]
    give_ref[CELLS:, :] = back0_ref[...]


def spread_kernel(terms_ref, out_ref):
    total = terms_ref[0]
    for k in range(1, terms_ref.shape[0]):
        total += terms_ref[k]
    for k in range(out_ref.shape[0]):
        out_ref[k] = total


def add_kernel(keep_ref, taken_ref, out_ref):
    out_ref[...] = keep_ref[...] + taken_ref[:CELLS, :]


def node_kernel(
    lists_ref,
    first_ref,
    mid_ref,
    second_ref,
    base_ref,
    own_ref,
    got_ref,
    weight_ref,
    out_ref,
    index_ref,
):
    back = jnp.concatenate([first_ref[...], mid_ref[...], second_ref[...]], axis=0)
    sent = own_ref[...] + fold(mul_rows(list_rows(lists_ref, index_ref), split(back)))
    value = mul(split(sent), mix(jnp.transpose(weight_ref[HID : 2 * HID, :])))
    value += mul(split(got_ref[...]), mix(jnp.transpose(weight_ref[2 * HID :, :])))
    out_ref[...] = base_ref[...] + fold(value)


def finish_kernel(
    part_ref, other_ref, ein_ref, eout_ref, nin_ref, nout_ref, eb, eg, nb, ng, *, scale
):
    mine = parity(2) == 0
    part, other = part_ref[...] * scale, other_ref[...] * scale
    low = jnp.where(mine, part, other)
    high = jnp.where(mine, other, part)
    ein_ref[...] = low[: 3 * HID]
    eout_ref[...] = low[3 * HID :]
    nin_ref[...] = high[: 2 * HID]
    nout_ref[...] = high[2 * HID : 3 * HID]
    for k, ref in enumerate((eb, eg, nb, ng)):
        ref[...] = high[3 * HID + k : 3 * HID + k + 1]


def call(body, outs, ins, scratch=(), smem=(), flops=0, limit=12):
    outs = [out if isinstance(out[0], tuple) else (out, F32) for out in outs]
    shapes = [jax.ShapeDtypeStruct(shape, kind) for shape, kind in outs]
    size = 4 * sum(math.prod(shape) for shape, _ in outs) + sum(4 * v.size for v in ins)
    return pl.pallas_call(
        body,
        out_shape=shapes,
        in_specs=[SMEM] * len(smem) + [VMEM] * len(ins),
        out_specs=[VMEM] * len(outs),
        scratch_shapes=[pltpu.VMEM(shape, kind) for shape, kind in scratch],
        cost_estimate=pl.CostEstimate(flops=flops, bytes_accessed=size, transcendentals=0),
        compiler_params=pltpu.CompilerParams(vmem_limit_bytes=limit * 1024 * 1024),
    )(*smem, *ins)


def make_packets(node_feat, lists):
    return call(
        packet_kernel,
        [(SLAB, HID)] * 3,
        [node_feat, lists],
        scratch=[((SLOT, HID), jnp.int32)],
        flops=10**9,
    )


def regroup(pieces, chunk, flops=0):
    body = functools.partial(regroup_kernel, chunk=chunk)
    return call(body, [(SLAB, HID)] * 3, pieces, flops=flops)


def edge_before(*operands):
    wide = (EDGES, HID)
    return call(
        before_kernel,
        [
            wide,
            (CELLS, HID),
            (wide, jnp.int32),
            (wide, jnp.int32),
            ((EDGES // HID, HID), jnp.int32),
            ((9, 2 * HID, 2 * HID), BF16),
        ],
        operands,
        flops=3 * 10**9,
        limit=20,
    )


def main_step(count, operands):
    square = (2 * HID, 2 * HID)
    wide = (EDGES, HID)
    return call(
        main_kernel,
        [(SLAB, HID)] * 3 + [(CELLS, HID)] * 3 + [wide, (2, *square), (CELLS, HID)],
        operands,
        scratch=[
            ((EDGES, 2 * HID), BF16),
            (wide, F32),
            (wide, F32),
            (wide, F32),
            ((CELLS, 2 * HID), F32),
            ((HALO, 2 * HID), BF16),
            ((CELLS + HALO, 2 * HID), F32),
        ],
        smem=[count],
        flops=10**10,
        limit=28,
    )


def weight_step(*operands):
    return call(
        weight_kernel,
        [(CELLS, HID), (CELLS + SLAB, HID)],
        operands,
        scratch=[((2, CELLS, HID), F32)],
        flops=1000000000,
    )


def node_after(*operands):
    return call(
        node_kernel,
        [(CELLS, HID)],
        operands,
        scratch=[((SLOT, HID), jnp.int32)],
        flops=1000000000000,
    )[0]


def finish(part, other, scale):
    shapes = [(3 * HID, HID), (HID, HID), (2 * HID, HID), (HID, HID)] + [(1, HID)] * 4
    return call(
        functools.partial(finish_kernel, scale=scale), shapes, [part, other], flops=10**6
    )


def swaps(axis):
    peers = lax.axis_size(axis)
    pairs = [[(i, i + 1) for i in range(start, peers - 1, 2)] for start in (0, 1)]
    return [sorted(some + [(j, i) for i, j in some]) for some in pairs]


def trade(first, second, axis):
    near, far = swaps(axis)
    second = lax.ppermute(second, axis, far)
    return lax.ppermute(first, axis, near), second


def join(values):
    return lax.optimization_barrier(values)


def sum_spread(terms, copies):
    return call(spread_kernel, [(copies, *terms.shape[1:])], [terms])[0]


def scatter_half(part):
    return lax.all_to_all(part.reshape(32, 16, HID), ("x", "zl", "zh"), 0, 0)


def every_term(terms):
    return lax.all_to_all(sum_spread(terms, 8), "y", 0, 0)


def gather_half(terms):
    part = lax.all_to_all(sum_spread(terms, 32), ("x", "zl", "zh"), 0, 0)
    return part.reshape(CELLS, HID)


def on_device(
    node_feat,
    edge_feat,
    node_cot,
    edge_cot,
    sender,
    receiver,
    block_count,
    send_rows,
    edge_in_weight,
    edge_bias,
    edge_out_weight,
    edge_gain,
    node_in_weight,
    node_bias,
    node_out_weight,
    node_gain,
):
    scale = 1.0 / math.sqrt(lax.axis_size(AXES) * EDGES)
    sender = sender.reshape(EDGES // HID, HID)
    receiver = receiver.reshape(EDGES // HID, HID)
    edge_bias, edge_gain, node_bias, node_gain = (
        row.reshape(1, HID) for row in (edge_bias, edge_gain, node_bias, node_gain)
    )
    first, mid, second = make_packets(node_feat, send_rows)
    first, second = trade(first, second, GX)
    before = edge_before(
        node_feat,
        edge_feat,
        sender,
        receiver,
        edge_in_weight,
        edge_bias,
        edge_out_weight,
        node_in_weight,
        node_bias,
        node_out_weight,
    )
    second, first, before = join((second, first, before))
    first, mid, second = regroup((first, mid, second), 3 * SLOT)
    first, second = trade(first, second, GY)
    first, mid, second = regroup((first, mid, second), SLOT)
    first, second = trade(first, second, GZ)
    second, first = join((second, first))
    halo = (first, mid, second)
    rest = (receiver, node_feat, node_cot, edge_cot, edge_feat, edge_gain, node_gain)
    *back, own, got, base, edge_grad, square, rows = main_step(block_count, (*halo, *before, *rest))
    keep, give = weight_step(node_feat, *halo, *back, own, got, square, rows)
    taken = lax.ppermute(give, "c", SWAP)
    part = call(add_kernel, [(CELLS, HID)], [keep, taken])[0]
    part = scatter_half(part)
    second = lax.ppermute(back[2], GZ, swaps(GZ)[1])
    first, mid, second = regroup((taken, back[1], second), SLOT, 1000000000000)
    part, _ = join((part, mid))
    part = every_term(part)
    first, second = trade(first, second, GY)
    first, mid, second = regroup((first, mid, second), 3 * SLOT, 0)
    part, first, mid, second = join((part, first, mid, second))
    part = gather_half(part)
    first, second = trade(first, second, GX)
    second, first = join((second, first))
    node_grad = node_after(
        send_rows, first, mid, second, base, own, got, edge_in_weight
    )
    part, node_grad = join((part, node_grad))
    other = lax.ppermute(part, "c", SWAP)
    ein, eout, nin, nout, eb, eg, nb, ng = finish(part, other, scale)
    vectors = [row.reshape(HID) for row in (eb, eg, nb, ng)]
    return (
        node_grad,
        edge_grad,
        ein,
        vectors[0],
        eout,
        vectors[1],
        nin,
        vectors[2],
        nout,
        vectors[3],
    )


def solution(mesh):
    fine = jax.sharding.Mesh(mesh.devices.reshape(SPLIT), AXES)
    return jax.shard_map(
        on_device,
        mesh=fine,
        in_specs=(
            P(AXES, None),
            P(AXES, None),
            P(AXES, None),
            P(AXES, None),
            P(AXES),
            P(AXES),
            P(AXES),
            P(GX, GY, GZ, None),
            P(),
            P(),
            P(),
            P(),
            P(),
            P(),
            P(),
            P(),
        ),
        out_specs=(
            P(AXES, None),
            P(AXES, None),
            P(),
            P(),
            P(),
            P(),
            P(),
            P(),
            P(),
            P(),
        ),
        check_vma=False,
    )
```

```python
import functools
import math

import jax
import jax.numpy as jnp
from jax import lax
from jax.experimental import pallas as pl
from jax.experimental.pallas import tpu as pltpu
from jax.sharding import PartitionSpec as P

NORM_EPS = 1e-05
AXES = ("y", "zl", "x", "zh", "c")
SPLIT = (8, 4, 4, 2, 2)
GX, GY, GZ = (("y", "zl"), ("x",), ("zh", "c"))
SWAP = [(0, 1), (1, 0)]
HID, CELLS, EDGES, SLOT = 128, 512, 2048, 32
SLAB = 9 * SLOT
HALO = 896
BLOCK = 512
F32, BF16 = jnp.float32, jnp.bfloat16
VMEM = pl.BlockSpec(memory_space=pltpu.VMEM)
SMEM = pl.BlockSpec(memory_space=pltpu.SMEM)


def split(value):
    high = value.astype(BF16)
    low = (value - high.astype(F32)).astype(BF16)
    return jnp.concatenate([high, low], axis=1)


def fold(value):
    return value[:, :HID] + value[:, HID:]


def mix(weight):
    high = weight.astype(BF16)
    low = (weight - high.astype(F32)).astype(BF16)
    top = jnp.concatenate([high, low], axis=1)
    bottom = jnp.concatenate([high, jnp.zeros_like(low)], axis=1)
    return jnp.concatenate([top, bottom], axis=0)


def mul(left, right):
    return jnp.dot(left, right, preferred_element_type=F32)


def mul_rows(left, right):
    return lax.dot_general(left, right, (((0,), (0,)), ((), ())), preferred_element_type=F32)


def quad(value):
    top, bottom = value[:HID], value[HID:]
    return fold(top) + fold(bottom)


def centred(weight):
    return weight - jnp.mean(weight, axis=1, keepdims=True)


def silu_parts(preact):
    gate = 1.0 / (1.0 + jnp.exp(-preact))
    hidden = preact * gate
    return hidden, gate + hidden * (1.0 - gate)


def spread_columns(index, out_ref):
    turned = jnp.transpose(index.astype(F32)).astype(jnp.int32)
    for block in range(EDGES // HID):
        column = turned[:, block : block + 1]
        out_ref[block * HID : (block + 1) * HID, :] = jnp.broadcast_to(column, (HID, HID))


def hot_rows(column, width, base=0):
    lane = lax.broadcasted_iota(jnp.int32, column.shape, 1)
    parts = [
        (column == lane + (base + start)).astype(F32).astype(BF16) for start in range(0, width, HID)
    ]
    return jnp.concatenate(parts, axis=1)


def hot_columns(ref, first, height, base=0):
    level = lax.broadcasted_iota(jnp.int32, (height, HID), 0) + base
    parts = []
    for j in range(BLOCK // HID):
        row = ref[pl.ds(first + j, 1), :]
        parts.append((level == row).astype(F32).astype(BF16))
    return jnp.concatenate(parts, axis=1)


def parity(dim):
    return lax.axis_index(("zl", "x", "c")[dim]) & 1


def near_first(odd, entry):
    return entry if entry == 1 else jnp.where(odd == 0, 2 - entry, entry)


def list_rows(lists_ref, index_ref):
    index_ref[...] = jnp.zeros_like(index_ref)
    for k in range(27):
        x, y, z = (
            near_first(parity(dim), entry) for dim, entry in enumerate((k // 9, k // 3 % 3, k % 3))
        )
        index_ref[k : k + 1, :SLOT] = lists_ref[x, y, pl.ds(z, 1), :]
    turned = jnp.transpose(index_ref[...].astype(F32)).astype(jnp.int32)
    cell = lax.broadcasted_iota(jnp.int32, (SLOT, CELLS), 1)
    parts = []
    for k in range(27):
        hot = (turned[:SLOT, k : k + 1] == cell).astype(F32)
        parts.append((hot if k != 13 else hot * 0.0).astype(BF16))
    return jnp.concatenate(parts, axis=0)


def packet_kernel(node_ref, lists_ref, first_ref, mid_ref, second_ref, index_ref):
    rows = fold(mul(list_rows(lists_ref, index_ref), split(node_ref[...])))
    first_ref[...] = rows[:SLAB]
    mid_ref[...] = rows[SLAB : 2 * SLAB]
    second_ref[...] = rows[2 * SLAB :]


def regroup_kernel(in0, in1, in2, out0, out1, out2, *, chunk):
    for i, source in enumerate((in0, in1, in2)):
        base = source.shape[0] - SLAB if i == 0 else 0
        for j, target in enumerate((out0, out1, out2)):
            for k in range(SLAB // (3 * chunk)):
                to = (3 * k + i) * chunk
                at = base + (3 * k + j) * chunk
                target[to : to + chunk, :] = source[at : at + chunk, :]


def before_kernel(
    node_ref,
    edge_ref,
    sender_ref,
    receiver_ref,
    ein_ref,
    ebias_ref,
    eout_ref,
    nin_ref,
    nbias_ref,
    nout_ref,
    pre_ref,
    node_pre_ref,
    send_ref,
    recv_ref,
    order_ref,
    mix_ref,
):
    raw = sender_ref[...]
    slot = raw - CELLS
    direction = slot >> 5
    third = (direction * 43) >> 7
    ninth = (third * 43) >> 7
    x, y, z = (
        2 - entry + parity(dim) * (2 * entry - 2)
        for dim, entry in enumerate((ninth, third - 3 * ninth, direction - 3 * third))
    )
    moved = CELLS + SLAB * z + SLOT * (3 * x + y) + (slot & (SLOT - 1))
    order_ref[...] = jnp.where(raw < CELLS, raw, moved)
    spread_columns(order_ref[...], send_ref)
    spread_columns(receiver_ref[...], recv_ref)
    own = split(node_ref[...])
    halo_mix = mix(ein_ref[HID : 2 * HID, :])
    sent = fold(mul(own, halo_mix))
    got = fold(mul(own, mix(ein_ref[2 * HID :, :])))
    table = jnp.concatenate([split(sent), split(got)], axis=0)
    first = mix(ein_ref[:HID, :])
    for i in range(EDGES // BLOCK):
        rows = slice(i * BLOCK, (i + 1) * BLOCK)
        hot = jnp.concatenate(
            [hot_rows(send_ref[rows, :], CELLS), hot_rows(recv_ref[rows, :], CELLS)], axis=1
        )
        value = mul(hot, table) + mul(split(edge_ref[rows, :]), first)
        pre_ref[rows, :] = fold(value) + ebias_ref[...]
    node_pre_ref[...] = fold(mul(own, mix(nin_ref[:HID, :]))) + nbias_ref[...]
    edge_out, node_out = centred(eout_ref[...]), centred(nout_ref[...])
    mix_ref[0] = halo_mix
    mix_ref[1] = mix(edge_out)
    mix_ref[2] = mix(jnp.transpose(edge_out))
    mix_ref[3] = mix(nin_ref[HID:, :])
    mix_ref[4] = mix(node_out)
    mix_ref[5] = mix(jnp.transpose(node_out))
    mix_ref[6] = mix(jnp.transpose(nin_ref[:HID, :]))
    mix_ref[7] = mix(jnp.transpose(nin_ref[HID:, :]))
    mix_ref[8] = mix(jnp.transpose(ein_ref[:HID, :]))


def main_kernel(
    count_ref,
    halo0_ref,
    halo1_ref,
    halo2_ref,
    pre_ref,
    node_pre_ref,
    send_ref,
    recv_ref,
    order_ref,
    mix_ref,
    receiver_ref,
    node_ref,
    node_cot_ref,
    cot_ref,
    edge_ref,
    egain_ref,
    ngain_ref,
    back0_ref,
    back1_ref,
    back2_ref,
    own_ref,
    got_ref,
    base_ref,
    edge_grad_ref,
    acc_ref,
    rest_ref,
    hid_ref,
    slope_ref,
    norm_ref,
    inv_ref,
    sum_ref,
    table_ref,
    row_ref,
):
    halo = [halo0_ref[...], halo1_ref[...], halo2_ref[...], jnp.zeros((HALO - 3 * SLAB, HID), F32)]
    halo_split = split(jnp.concatenate(halo, axis=0))
    table_ref[...] = split(fold(mul(halo_split, mix_ref[0])))
    gain = egain_ref[...]

    def live(i):
        row = lax.broadcasted_iota(jnp.int32, (HID, HID), 0)
        blocks = BLOCK // HID
        return jnp.concatenate([row < count_ref[i * blocks + j] for j in range(blocks)], axis=0)

    for i in range(EDGES // BLOCK):
        rows = slice(i * BLOCK, (i + 1) * BLOCK)
        hot = hot_rows(send_ref[rows, :], HALO, CELLS)
        preact = pre_ref[rows, :] + fold(mul(hot, table_ref[...]))
        hidden, slope = silu_parts(preact)
        hidden = split(hidden)
        hid_ref[rows, :] = hidden
        slope_ref[rows, :] = slope
        value = fold(mul(hidden, mix_ref[1]))
        inv = lax.rsqrt(jnp.mean(value * value, axis=1, keepdims=True) + NORM_EPS)
        norm = value * inv
        norm_ref[rows, :] = norm
        inv_ref[rows, :] = jnp.broadcast_to(inv, norm.shape)
        message = jnp.where(live(i), norm * gain, 0.0)
        term = mul(hot_columns(receiver_ref, i * (BLOCK // HID), CELLS), split(message))
        sum_ref[...] = term if i == 0 else sum_ref[...] + term

    node_split = split(node_ref[...])
    summed = split(fold(sum_ref[...]))
    hidden, slope = silu_parts(node_pre_ref[...] + fold(mul(summed, mix_ref[3])))
    hidden = split(hidden)
    value = fold(mul(hidden, mix_ref[4]))
    inv = lax.rsqrt(jnp.mean(value * value, axis=1, keepdims=True) + NORM_EPS)
    norm = value * inv
    cot = node_cot_ref[...]
    dnorm = cot * ngain_ref[...]
    dvalue = split(inv * (dnorm - norm * jnp.mean(dnorm * norm, axis=1, keepdims=True)))
    dpre = fold(mul(dvalue, mix_ref[5])) * slope
    dpre_split = split(dpre)
    table_ref[:CELLS, :] = split(fold(mul(dpre_split, mix_ref[7])))
    base_ref[...] = cot + fold(mul(dpre_split, mix_ref[6]))
    rest_ref[0:HID, :] = quad(mul_rows(node_split, dpre_split))
    rest_ref[HID : 2 * HID, :] = quad(mul_rows(summed, dpre_split))
    rest_ref[2 * HID : 3 * HID, :] = centred(quad(mul_rows(hidden, dvalue)))
    rest_ref[3 * HID :, :] = jnp.zeros((HID, HID), F32)
    rest_ref[3 * HID + 2 : 3 * HID + 3, :] = jnp.sum(dpre, axis=0, keepdims=True)
    rest_ref[3 * HID + 3 : 3 * HID + 4, :] = jnp.sum(cot * norm, axis=0, keepdims=True)

    bias_grad = gain_grad = jnp.zeros((1, HID), F32)
    for i in range(EDGES // BLOCK):
        rows = slice(i * BLOCK, (i + 1) * BLOCK)
        hot = hot_rows(recv_ref[rows, :], CELLS)
        grad = cot_ref[rows, :] + fold(mul(hot, table_ref[:CELLS, :]))
        grad = jnp.where(live(i), grad, 0.0)
        norm = norm_ref[rows, :]
        dnorm = grad * gain
        dvalue = inv_ref[rows, :] * (dnorm - norm * jnp.mean(dnorm * norm, axis=1, keepdims=True))
        dvalue = split(dvalue)
        dpre = fold(mul(dvalue, mix_ref[2])) * slope_ref[rows, :]
        dpre_split = split(dpre)
        edge_grad_ref[rows, :] = cot_ref[rows, :] + fold(mul(dpre_split, mix_ref[8]))
        first = i * (BLOCK // HID)
        terms = (
            mul(hot_columns(order_ref, first, CELLS + HALO), dpre_split),
            mul(hot_columns(receiver_ref, first, CELLS), dpre_split),
            mul_rows(hid_ref[rows, :], dvalue),
            mul_rows(split(edge_ref[rows, :]), dpre_split),
        )
        targets = (row_ref, sum_ref, acc_ref.at[0], acc_ref.at[1])
        for target, term in zip(targets, terms):
            target[...] = term if i == 0 else target[...] + term
        bias_grad += jnp.sum(dpre, axis=0, keepdims=True)
        gain_grad += jnp.sum(grad * norm, axis=0, keepdims=True)
    own_ref[...] = fold(row_ref[:CELLS, :])
    got_ref[...] = fold(sum_ref[...])
    for k, ref in enumerate((back0_ref, back1_ref, back2_ref)):
        start = CELLS + k * SLAB
        ref[...] = fold(row_ref[start : start + SLAB, :])
    rest_ref[3 * HID : 3 * HID + 1, :] = bias_grad
    rest_ref[3 * HID + 1 : 3 * HID + 2, :] = gain_grad


def weight_kernel(
    node_ref,
    halo0_ref,
    halo1_ref,
    halo2_ref,
    back0_ref,
    back1_ref,
    back2_ref,
    own_ref,
    got_ref,
    acc_ref,
    rest_ref,
    keep_ref,
    give_ref,
    grads_ref,
):
    node_split = split(node_ref[...])
    sent = quad(mul_rows(node_split, split(own_ref[...])))
    for halo, back in ((halo0_ref, back0_ref), (halo1_ref, back1_ref), (halo2_ref, back2_ref)):
        sent += quad(mul_rows(split(halo[...]), split(back[...])))
    grads_ref[0, 0:HID, :] = quad(acc_ref[1])
    grads_ref[0, HID : 2 * HID, :] = sent
    grads_ref[0, 2 * HID : 3 * HID, :] = quad(mul_rows(node_split, split(got_ref[...])))
    grads_ref[0, 3 * HID :, :] = centred(quad(acc_ref[0]))
    grads_ref[1] = rest_ref[...]
    side = parity(2)
    keep_ref[...] = grads_ref[side]
    give_ref[:CELLS, :] = grads_ref[1 - side]
    give_ref[CELLS:, :] = back0_ref[...]


def spread_kernel(terms_ref, out_ref):
    total = terms_ref[0]
    for k in range(1, terms_ref.shape[0]):
        total += terms_ref[k]
    for k in range(out_ref.shape[0]):
        out_ref[k] = total


def add_kernel(keep_ref, taken_ref, out_ref):
    out_ref[...] = keep_ref[...] + taken_ref[:CELLS, :]


def node_kernel(
    lists_ref,
    first_ref,
    mid_ref,
    second_ref,
    base_ref,
    own_ref,
    got_ref,
    weight_ref,
    out_ref,
    index_ref,
):
    back = jnp.concatenate([first_ref[...], mid_ref[...], second_ref[...]], axis=0)
    sent = own_ref[...] + fold(mul_rows(list_rows(lists_ref, index_ref), split(back)))
    value = mul(split(sent), mix(jnp.transpose(weight_ref[HID : 2 * HID, :])))
    value += mul(split(got_ref[...]), mix(jnp.transpose(weight_ref[2 * HID :, :])))
    out_ref[...] = base_ref[...] + fold(value)


def finish_kernel(
    part_ref, other_ref, ein_ref, eout_ref, nin_ref, nout_ref, eb, eg, nb, ng, *, scale
):
    mine = parity(2) == 0
    part, other = part_ref[...] * scale, other_ref[...] * scale
    low = jnp.where(mine, part, other)
    high = jnp.where(mine, other, part)
    ein_ref[...] = low[: 3 * HID]
    eout_ref[...] = low[3 * HID :]
    nin_ref[...] = high[: 2 * HID]
    nout_ref[...] = high[2 * HID : 3 * HID]
    for k, ref in enumerate((eb, eg, nb, ng)):
        ref[...] = high[3 * HID + k : 3 * HID + k + 1]


def call(body, outs, ins, scratch=(), smem=(), flops=0, limit=12):
    outs = [out if isinstance(out[0], tuple) else (out, F32) for out in outs]
    shapes = [jax.ShapeDtypeStruct(shape, kind) for shape, kind in outs]
    size = 4 * sum(math.prod(shape) for shape, _ in outs) + sum(4 * v.size for v in ins)
    return pl.pallas_call(
        body,
        out_shape=shapes,
        in_specs=[SMEM] * len(smem) + [VMEM] * len(ins),
        out_specs=[VMEM] * len(outs),
        scratch_shapes=[pltpu.VMEM(shape, kind) for shape, kind in scratch],
        cost_estimate=pl.CostEstimate(flops=flops, bytes_accessed=size, transcendentals=0),
        compiler_params=pltpu.CompilerParams(vmem_limit_bytes=limit * 1024 * 1024),
    )(*smem, *ins)


def make_packets(node_feat, lists):
    return call(
        packet_kernel,
        [(SLAB, HID)] * 3,
        [node_feat, lists],
        scratch=[((SLOT, HID), jnp.int32)],
        flops=10**9,
    )


def regroup(pieces, chunk, flops=0):
    body = functools.partial(regroup_kernel, chunk=chunk)
    return call(body, [(SLAB, HID)] * 3, pieces, flops=flops)


def edge_before(*operands):
    wide = (EDGES, HID)
    return call(
        before_kernel,
        [
            wide,
            (CELLS, HID),
            (wide, jnp.int32),
            (wide, jnp.int32),
            ((EDGES // HID, HID), jnp.int32),
            ((9, 2 * HID, 2 * HID), BF16),
        ],
        operands,
        flops=3 * 10**9,
        limit=20,
    )


def main_step(count, operands):
    square = (2 * HID, 2 * HID)
    wide = (EDGES, HID)
    return call(
        main_kernel,
        [(SLAB, HID)] * 3 + [(CELLS, HID)] * 3 + [wide, (2, *square), (CELLS, HID)],
        operands,
        scratch=[
            ((EDGES, 2 * HID), BF16),
            (wide, F32),
            (wide, F32),
            (wide, F32),
            ((CELLS, 2 * HID), F32),
            ((HALO, 2 * HID), BF16),
            ((CELLS + HALO, 2 * HID), F32),
        ],
        smem=[count],
        flops=10**10,
        limit=28,
    )


def weight_step(*operands):
    return call(
        weight_kernel,
        [(CELLS, HID), (CELLS + SLAB, HID)],
        operands,
        scratch=[((2, CELLS, HID), F32)],
        flops=1000000000,
    )


def node_after(*operands):
    return call(
        node_kernel,
        [(CELLS, HID)],
        operands,
        scratch=[((SLOT, HID), jnp.int32)],
        flops=5 * 10**9,
    )[0]


def finish(part, other, scale):
    shapes = [(3 * HID, HID), (HID, HID), (2 * HID, HID), (HID, HID)] + [(1, HID)] * 4
    return call(
        functools.partial(finish_kernel, scale=scale), shapes, [part, other], flops=10**6
    )


def swaps(axis):
    peers = lax.axis_size(axis)
    pairs = [[(i, i + 1) for i in range(start, peers - 1, 2)] for start in (0, 1)]
    return [sorted(some + [(j, i) for i, j in some]) for some in pairs]


def trade(first, second, axis):
    near, far = swaps(axis)
    second = lax.ppermute(second, axis, far)
    return lax.ppermute(first, axis, near), second


def join(values):
    return lax.optimization_barrier(values)


def sum_spread(terms, copies):
    return call(spread_kernel, [(copies, *terms.shape[1:])], [terms])[0]


def scatter_half(part):
    return lax.all_to_all(part.reshape(32, 16, HID), ("x", "zl", "zh"), 0, 0)


def every_term(terms):
    return lax.all_to_all(sum_spread(terms, 8), "y", 0, 0)


def gather_half(terms):
    part = lax.all_to_all(sum_spread(terms, 32), ("x", "zl", "zh"), 0, 0)
    return part.reshape(CELLS, HID)


def on_device(
    node_feat,
    edge_feat,
    node_cot,
    edge_cot,
    sender,
    receiver,
    block_count,
    send_rows,
    edge_in_weight,
    edge_bias,
    edge_out_weight,
    edge_gain,
    node_in_weight,
    node_bias,
    node_out_weight,
    node_gain,
):
    scale = 1.0 / math.sqrt(lax.axis_size(AXES) * EDGES)
    sender = sender.reshape(EDGES // HID, HID)
    receiver = receiver.reshape(EDGES // HID, HID)
    edge_bias, edge_gain, node_bias, node_gain = (
        row.reshape(1, HID) for row in (edge_bias, edge_gain, node_bias, node_gain)
    )
    first, mid, second = make_packets(node_feat, send_rows)
    first, second = trade(first, second, GX)
    before = edge_before(
        node_feat,
        edge_feat,
        sender,
        receiver,
        edge_in_weight,
        edge_bias,
        edge_out_weight,
        node_in_weight,
        node_bias,
        node_out_weight,
    )
    second, first, before = join((second, first, before))
    first, mid, second = regroup((first, mid, second), 3 * SLOT)
    first, second = trade(first, second, GY)
    first, mid, second = regroup((first, mid, second), SLOT)
    first, second = trade(first, second, GZ)
    second, first = join((second, first))
    halo = (first, mid, second)
    rest = (receiver, node_feat, node_cot, edge_cot, edge_feat, edge_gain, node_gain)
    *back, own, got, base, edge_grad, square, rows = main_step(block_count, (*halo, *before, *rest))
    keep, give = weight_step(node_feat, *halo, *back, own, got, square, rows)
    taken = lax.ppermute(give, "c", SWAP)
    part = call(add_kernel, [(CELLS, HID)], [keep, taken])[0]
    part = scatter_half(part)
    second = lax.ppermute(back[2], GZ, swaps(GZ)[1])
    first, mid, second = regroup((taken, back[1], second), SLOT, 10**10)
    part, _ = join((part, mid))
    part = every_term(part)
    first, second = trade(first, second, GY)
    first, mid, second = regroup((first, mid, second), 3 * SLOT, 0)
    part, _ = join((part, mid))
    part = gather_half(part)
    first, second = trade(first, second, GX)
    second, first = join((second, first))
    node_grad = node_after(
        send_rows, first, mid, second, base, own, got, edge_in_weight
    )
    part, node_grad = join((part, node_grad))
    other = lax.ppermute(part, "c", SWAP)
    ein, eout, nin, nout, eb, eg, nb, ng = finish(part, other, scale)
    vectors = [row.reshape(HID) for row in (eb, eg, nb, ng)]
    return (
        node_grad,
        edge_grad,
        ein,
        vectors[0],
        eout,
        vectors[1],
        nin,
        vectors[2],
        nout,
        vectors[3],
    )


def solution(mesh):
    fine = jax.sharding.Mesh(mesh.devices.reshape(SPLIT), AXES)
    return jax.shard_map(
        on_device,
        mesh=fine,
        in_specs=(
            P(AXES, None),
            P(AXES, None),
            P(AXES, None),
            P(AXES, None),
            P(AXES),
            P(AXES),
            P(AXES),
            P(GX, GY, GZ, None),
            P(),
            P(),
            P(),
            P(),
            P(),
            P(),
            P(),
            P(),
        ),
        out_specs=(
            P(AXES, None),
            P(AXES, None),
            P(),
            P(),
            P(),
            P(),
            P(),
            P(),
            P(),
            P(),
        ),
        check_vma=False,
    )
```

```python
import functools
import math

import jax
import jax.numpy as jnp
from jax import lax
from jax.experimental import pallas as pl
from jax.experimental.pallas import tpu as pltpu
from jax.sharding import PartitionSpec as P

NORM_EPS = 1e-05
AXES = ("y", "zl", "x", "zh", "c")
SPLIT = (8, 4, 4, 2, 2)
GX, GY, GZ = (("y", "zl"), ("x",), ("zh", "c"))
SWAP = [(0, 1), (1, 0)]
HID, CELLS, EDGES, SLOT = 128, 512, 2048, 32
SLAB = 9 * SLOT
HALO = 896
BLOCK = 512
F32, BF16 = jnp.float32, jnp.bfloat16
VMEM = pl.BlockSpec(memory_space=pltpu.VMEM)
SMEM = pl.BlockSpec(memory_space=pltpu.SMEM)


def split(value):
    high = value.astype(BF16)
    low = (value - high.astype(F32)).astype(BF16)
    return jnp.concatenate([high, low], axis=1)


def fold(value):
    return value[:, :HID] + value[:, HID:]


def mix(weight):
    high = weight.astype(BF16)
    low = (weight - high.astype(F32)).astype(BF16)
    top = jnp.concatenate([high, low], axis=1)
    bottom = jnp.concatenate([high, jnp.zeros_like(low)], axis=1)
    return jnp.concatenate([top, bottom], axis=0)


def mul(left, right):
    return jnp.dot(left, right, preferred_element_type=F32)


def mul_rows(left, right):
    return lax.dot_general(left, right, (((0,), (0,)), ((), ())), preferred_element_type=F32)


def quad(value):
    top, bottom = value[:HID], value[HID:]
    return fold(top) + fold(bottom)


def centred(weight):
    return weight - jnp.mean(weight, axis=1, keepdims=True)


def silu_parts(preact):
    gate = 1.0 / (1.0 + jnp.exp(-preact))
    hidden = preact * gate
    return hidden, gate + hidden * (1.0 - gate)


def spread_columns(index, out_ref):
    turned = jnp.transpose(index.astype(F32)).astype(jnp.int32)
    for block in range(EDGES // HID):
        column = turned[:, block : block + 1]
        out_ref[block * HID : (block + 1) * HID, :] = jnp.broadcast_to(column, (HID, HID))


def hot_rows(column, width, base=0):
    lane = lax.broadcasted_iota(jnp.int32, column.shape, 1)
    parts = [
        (column == lane + (base + start)).astype(F32).astype(BF16) for start in range(0, width, HID)
    ]
    return jnp.concatenate(parts, axis=1)


def hot_columns(ref, first, height, base=0):
    level = lax.broadcasted_iota(jnp.int32, (height, HID), 0) + base
    parts = []
    for j in range(BLOCK // HID):
        row = ref[pl.ds(first + j, 1), :]
        parts.append((level == row).astype(F32).astype(BF16))
    return jnp.concatenate(parts, axis=1)


def parity(dim):
    return lax.axis_index(("zl", "x", "c")[dim]) & 1


def near_first(odd, entry):
    return entry if entry == 1 else jnp.where(odd == 0, 2 - entry, entry)


def list_rows(lists_ref, index_ref):
    index_ref[...] = jnp.zeros_like(index_ref)
    for k in range(27):
        x, y, z = (
            near_first(parity(dim), entry) for dim, entry in enumerate((k // 9, k // 3 % 3, k % 3))
        )
        index_ref[k : k + 1, :SLOT] = lists_ref[x, y, pl.ds(z, 1), :]
    turned = jnp.transpose(index_ref[...].astype(F32)).astype(jnp.int32)
    cell = lax.broadcasted_iota(jnp.int32, (SLOT, CELLS), 1)
    parts = []
    for k in range(27):
        hot = (turned[:SLOT, k : k + 1] == cell).astype(F32)
        parts.append((hot if k != 13 else hot * 0.0).astype(BF16))
    return jnp.concatenate(parts, axis=0)


def packet_kernel(node_ref, lists_ref, first_ref, mid_ref, second_ref, index_ref):
    rows = fold(mul(list_rows(lists_ref, index_ref), split(node_ref[...])))
    first_ref[...] = rows[:SLAB]
    mid_ref[...] = rows[SLAB : 2 * SLAB]
    second_ref[...] = rows[2 * SLAB :]


def regroup_kernel(in0, in1, in2, out0, out1, out2, *, chunk):
    for i, source in enumerate((in0, in1, in2)):
        base = source.shape[0] - SLAB if i == 0 else 0
        for j, target in enumerate((out0, out1, out2)):
            for k in range(SLAB // (3 * chunk)):
                to = (3 * k + i) * chunk
                at = base + (3 * k + j) * chunk
                target[to : to + chunk, :] = source[at : at + chunk, :]


def before_kernel(
    node_ref,
    edge_ref,
    sender_ref,
    receiver_ref,
    ein_ref,
    ebias_ref,
    eout_ref,
    nin_ref,
    nbias_ref,
    nout_ref,
    pre_ref,
    node_pre_ref,
    send_ref,
    recv_ref,
    order_ref,
    mix_ref,
):
    raw = sender_ref[...]
    slot = raw - CELLS
    direction = slot >> 5
    third = (direction * 43) >> 7
    ninth = (third * 43) >> 7
    x, y, z = (
        2 - entry + parity(dim) * (2 * entry - 2)
        for dim, entry in enumerate((ninth, third - 3 * ninth, direction - 3 * third))
    )
    moved = CELLS + SLAB * z + SLOT * (3 * x + y) + (slot & (SLOT - 1))
    order_ref[...] = jnp.where(raw < CELLS, raw, moved)
    spread_columns(order_ref[...], send_ref)
    spread_columns(receiver_ref[...], recv_ref)
    own = split(node_ref[...])
    halo_mix = mix(ein_ref[HID : 2 * HID, :])
    sent = fold(mul(own, halo_mix))
    got = fold(mul(own, mix(ein_ref[2 * HID :, :])))
    table = jnp.concatenate([split(sent), split(got)], axis=0)
    first = mix(ein_ref[:HID, :])
    for i in range(EDGES // BLOCK):
        rows = slice(i * BLOCK, (i + 1) * BLOCK)
        hot = jnp.concatenate(
            [hot_rows(send_ref[rows, :], CELLS), hot_rows(recv_ref[rows, :], CELLS)], axis=1
        )
        value = mul(hot, table) + mul(split(edge_ref[rows, :]), first)
        pre_ref[rows, :] = fold(value) + ebias_ref[...]
    node_pre_ref[...] = fold(mul(own, mix(nin_ref[:HID, :]))) + nbias_ref[...]
    edge_out, node_out = centred(eout_ref[...]), centred(nout_ref[...])
    mix_ref[0] = halo_mix
    mix_ref[1] = mix(edge_out)
    mix_ref[2] = mix(jnp.transpose(edge_out))
    mix_ref[3] = mix(nin_ref[HID:, :])
    mix_ref[4] = mix(node_out)
    mix_ref[5] = mix(jnp.transpose(node_out))
    mix_ref[6] = mix(jnp.transpose(nin_ref[:HID, :]))
    mix_ref[7] = mix(jnp.transpose(nin_ref[HID:, :]))
    mix_ref[8] = mix(jnp.transpose(ein_ref[:HID, :]))


def main_kernel(
    count_ref,
    halo0_ref,
    halo1_ref,
    halo2_ref,
    pre_ref,
    node_pre_ref,
    send_ref,
    recv_ref,
    order_ref,
    mix_ref,
    receiver_ref,
    node_ref,
    node_cot_ref,
    cot_ref,
    edge_ref,
    egain_ref,
    ngain_ref,
    back0_ref,
    back1_ref,
    back2_ref,
    own_ref,
    got_ref,
    base_ref,
    edge_grad_ref,
    acc_ref,
    rest_ref,
    hid_ref,
    slope_ref,
    norm_ref,
    inv_ref,
    sum_ref,
    table_ref,
    row_ref,
):
    halo = [halo0_ref[...], halo1_ref[...], halo2_ref[...], jnp.zeros((HALO - 3 * SLAB, HID), F32)]
    halo_split = split(jnp.concatenate(halo, axis=0))
    table_ref[...] = split(fold(mul(halo_split, mix_ref[0])))
    gain = egain_ref[...]

    def live(i):
        row = lax.broadcasted_iota(jnp.int32, (HID, HID), 0)
        blocks = BLOCK // HID
        return jnp.concatenate([row < count_ref[i * blocks + j] for j in range(blocks)], axis=0)

    for i in range(EDGES // BLOCK):
        rows = slice(i * BLOCK, (i + 1) * BLOCK)
        hot = hot_rows(send_ref[rows, :], HALO, CELLS)
        preact = pre_ref[rows, :] + fold(mul(hot, table_ref[...]))
        hidden, slope = silu_parts(preact)
        hidden = split(hidden)
        hid_ref[rows, :] = hidden
        slope_ref[rows, :] = slope
        value = fold(mul(hidden, mix_ref[1]))
        inv = lax.rsqrt(jnp.mean(value * value, axis=1, keepdims=True) + NORM_EPS)
        norm = value * inv
        norm_ref[rows, :] = norm
        inv_ref[rows, :] = jnp.broadcast_to(inv, norm.shape)
        message = jnp.where(live(i), norm * gain, 0.0)
        term = mul(hot_columns(receiver_ref, i * (BLOCK // HID), CELLS), split(message))
        sum_ref[...] = term if i == 0 else sum_ref[...] + term

    node_split = split(node_ref[...])
    summed = split(fold(sum_ref[...]))
    hidden, slope = silu_parts(node_pre_ref[...] + fold(mul(summed, mix_ref[3])))
    hidden = split(hidden)
    value = fold(mul(hidden, mix_ref[4]))
    inv = lax.rsqrt(jnp.mean(value * value, axis=1, keepdims=True) + NORM_EPS)
    norm = value * inv
    cot = node_cot_ref[...]
    dnorm = cot * ngain_ref[...]
    dvalue = split(inv * (dnorm - norm * jnp.mean(dnorm * norm, axis=1, keepdims=True)))
    dpre = fold(mul(dvalue, mix_ref[5])) * slope
    dpre_split = split(dpre)
    table_ref[:CELLS, :] = split(fold(mul(dpre_split, mix_ref[7])))
    base_ref[...] = cot + fold(mul(dpre_split, mix_ref[6]))
    rest_ref[0:HID, :] = quad(mul_rows(node_split, dpre_split))
    rest_ref[HID : 2 * HID, :] = quad(mul_rows(summed, dpre_split))
    rest_ref[2 * HID : 3 * HID, :] = centred(quad(mul_rows(hidden, dvalue)))
    rest_ref[3 * HID :, :] = jnp.zeros((HID, HID), F32)
    rest_ref[3 * HID + 2 : 3 * HID + 3, :] = jnp.sum(dpre, axis=0, keepdims=True)
    rest_ref[3 * HID + 3 : 3 * HID + 4, :] = jnp.sum(cot * norm, axis=0, keepdims=True)

    bias_grad = gain_grad = jnp.zeros((1, HID), F32)
    for i in range(EDGES // BLOCK):
        rows = slice(i * BLOCK, (i + 1) * BLOCK)
        hot = hot_rows(recv_ref[rows, :], CELLS)
        grad = cot_ref[rows, :] + fold(mul(hot, table_ref[:CELLS, :]))
        grad = jnp.where(live(i), grad, 0.0)
        norm = norm_ref[rows, :]
        dnorm = grad * gain
        dvalue = inv_ref[rows, :] * (dnorm - norm * jnp.mean(dnorm * norm, axis=1, keepdims=True))
        dvalue = split(dvalue)
        dpre = fold(mul(dvalue, mix_ref[2])) * slope_ref[rows, :]
        dpre_split = split(dpre)
        edge_grad_ref[rows, :] = cot_ref[rows, :] + fold(mul(dpre_split, mix_ref[8]))
        first = i * (BLOCK // HID)
        terms = (
            mul(hot_columns(order_ref, first, CELLS + HALO), dpre_split),
            mul(hot_columns(receiver_ref, first, CELLS), dpre_split),
            mul_rows(hid_ref[rows, :], dvalue),
            mul_rows(split(edge_ref[rows, :]), dpre_split),
        )
        targets = (row_ref, sum_ref, acc_ref.at[0], acc_ref.at[1])
        for target, term in zip(targets, terms):
            target[...] = term if i == 0 else target[...] + term
        bias_grad += jnp.sum(dpre, axis=0, keepdims=True)
        gain_grad += jnp.sum(grad * norm, axis=0, keepdims=True)
    own_ref[...] = fold(row_ref[:CELLS, :])
    got_ref[...] = fold(sum_ref[...])
    for k, ref in enumerate((back0_ref, back1_ref, back2_ref)):
        start = CELLS + k * SLAB
        ref[...] = fold(row_ref[start : start + SLAB, :])
    rest_ref[3 * HID : 3 * HID + 1, :] = bias_grad
    rest_ref[3 * HID + 1 : 3 * HID + 2, :] = gain_grad


def weight_kernel(
    node_ref,
    halo0_ref,
    halo1_ref,
    halo2_ref,
    back0_ref,
    back1_ref,
    back2_ref,
    own_ref,
    got_ref,
    acc_ref,
    rest_ref,
    keep_ref,
    give_ref,
    grads_ref,
):
    node_split = split(node_ref[...])
    sent = quad(mul_rows(node_split, split(own_ref[...])))
    for halo, back in ((halo0_ref, back0_ref), (halo1_ref, back1_ref), (halo2_ref, back2_ref)):
        sent += quad(mul_rows(split(halo[...]), split(back[...])))
    grads_ref[0, 0:HID, :] = quad(acc_ref[1])
    grads_ref[0, HID : 2 * HID, :] = sent
    grads_ref[0, 2 * HID : 3 * HID, :] = quad(mul_rows(node_split, split(got_ref[...])))
    grads_ref[0, 3 * HID :, :] = centred(quad(acc_ref[0]))
    grads_ref[1] = rest_ref[...]
    side = parity(2)
    keep_ref[...] = grads_ref[side]
    give_ref[:CELLS, :] = grads_ref[1 - side]
    give_ref[CELLS:, :] = back0_ref[...]


def spread_kernel(terms_ref, out_ref):
    total = terms_ref[0]
    for k in range(1, terms_ref.shape[0]):
        total += terms_ref[k]
    for k in range(out_ref.shape[0]):
        out_ref[k] = total


def add_kernel(keep_ref, taken_ref, out_ref):
    out_ref[...] = keep_ref[...] + taken_ref[:CELLS, :]


def node_kernel(
    lists_ref,
    first_ref,
    mid_ref,
    second_ref,
    base_ref,
    own_ref,
    got_ref,
    weight_ref,
    out_ref,
    index_ref,
):
    back = jnp.concatenate([first_ref[...], mid_ref[...], second_ref[...]], axis=0)
    sent = own_ref[...] + fold(mul_rows(list_rows(lists_ref, index_ref), split(back)))
    value = mul(split(sent), mix(jnp.transpose(weight_ref[HID : 2 * HID, :])))
    value += mul(split(got_ref[...]), mix(jnp.transpose(weight_ref[2 * HID :, :])))
    out_ref[...] = base_ref[...] + fold(value)


def finish_kernel(
    part_ref, other_ref, ein_ref, eout_ref, nin_ref, nout_ref, eb, eg, nb, ng, *, scale
):
    mine = parity(2) == 0
    part, other = part_ref[...] * scale, other_ref[...] * scale
    low = jnp.where(mine, part, other)
    high = jnp.where(mine, other, part)
    ein_ref[...] = low[: 3 * HID]
    eout_ref[...] = low[3 * HID :]
    nin_ref[...] = high[: 2 * HID]
    nout_ref[...] = high[2 * HID : 3 * HID]
    for k, ref in enumerate((eb, eg, nb, ng)):
        ref[...] = high[3 * HID + k : 3 * HID + k + 1]


def call(body, outs, ins, scratch=(), smem=(), flops=0, limit=12):
    outs = [out if isinstance(out[0], tuple) else (out, F32) for out in outs]
    shapes = [jax.ShapeDtypeStruct(shape, kind) for shape, kind in outs]
    size = 4 * sum(math.prod(shape) for shape, _ in outs) + sum(4 * v.size for v in ins)
    return pl.pallas_call(
        body,
        out_shape=shapes,
        in_specs=[SMEM] * len(smem) + [VMEM] * len(ins),
        out_specs=[VMEM] * len(outs),
        scratch_shapes=[pltpu.VMEM(shape, kind) for shape, kind in scratch],
        cost_estimate=pl.CostEstimate(flops=flops, bytes_accessed=size, transcendentals=0),
        compiler_params=pltpu.CompilerParams(vmem_limit_bytes=limit * 1024 * 1024),
    )(*smem, *ins)


def make_packets(node_feat, lists):
    return call(
        packet_kernel,
        [(SLAB, HID)] * 3,
        [node_feat, lists],
        scratch=[((SLOT, HID), jnp.int32)],
        flops=10**9,
    )


def regroup(pieces, chunk, flops=0):
    body = functools.partial(regroup_kernel, chunk=chunk)
    return call(body, [(SLAB, HID)] * 3, pieces, flops=flops)


def edge_before(*operands):
    wide = (EDGES, HID)
    return call(
        before_kernel,
        [
            wide,
            (CELLS, HID),
            (wide, jnp.int32),
            (wide, jnp.int32),
            ((EDGES // HID, HID), jnp.int32),
            ((9, 2 * HID, 2 * HID), BF16),
        ],
        operands,
        flops=3 * 10**9,
        limit=20,
    )


def main_step(count, operands):
    square = (2 * HID, 2 * HID)
    wide = (EDGES, HID)
    return call(
        main_kernel,
        [(SLAB, HID)] * 3 + [(CELLS, HID)] * 3 + [wide, (2, *square), (CELLS, HID)],
        operands,
        scratch=[
            ((EDGES, 2 * HID), BF16),
            (wide, F32),
            (wide, F32),
            (wide, F32),
            ((CELLS, 2 * HID), F32),
            ((HALO, 2 * HID), BF16),
            ((CELLS + HALO, 2 * HID), F32),
        ],
        smem=[count],
        flops=10**10,
        limit=28,
    )


def weight_step(*operands):
    return call(
        weight_kernel,
        [(CELLS, HID), (CELLS + SLAB, HID)],
        operands,
        scratch=[((2, CELLS, HID), F32)],
        flops=1000000000,
    )


def node_after(*operands):
    return call(
        node_kernel,
        [(CELLS, HID)],
        operands,
        scratch=[((SLOT, HID), jnp.int32)],
        flops=5 * 10**9,
    )[0]


def finish(part, other, scale):
    shapes = [(3 * HID, HID), (HID, HID), (2 * HID, HID), (HID, HID)] + [(1, HID)] * 4
    return call(
        functools.partial(finish_kernel, scale=scale), shapes, [part, other], flops=10**6
    )


def swaps(axis):
    peers = lax.axis_size(axis)
    pairs = [[(i, i + 1) for i in range(start, peers - 1, 2)] for start in (0, 1)]
    return [sorted(some + [(j, i) for i, j in some]) for some in pairs]


def trade(first, second, axis):
    near, far = swaps(axis)
    second = lax.ppermute(second, axis, far)
    return lax.ppermute(first, axis, near), second


def join(values):
    return lax.optimization_barrier(values)


def sum_spread(terms, copies):
    return call(spread_kernel, [(copies, *terms.shape[1:])], [terms])[0]


def scatter_half(part):
    return lax.all_to_all(part.reshape(32, 16, HID), ("x", "y"), 0, 0)


def every_term(terms):
    return lax.all_to_all(sum_spread(terms, 8), ("zl", "zh"), 0, 0)


def gather_half(terms):
    part = lax.all_to_all(sum_spread(terms, 32), ("x", "y"), 0, 0)
    return part.reshape(CELLS, HID)


def on_device(
    node_feat,
    edge_feat,
    node_cot,
    edge_cot,
    sender,
    receiver,
    block_count,
    send_rows,
    edge_in_weight,
    edge_bias,
    edge_out_weight,
    edge_gain,
    node_in_weight,
    node_bias,
    node_out_weight,
    node_gain,
):
    scale = 1.0 / math.sqrt(lax.axis_size(AXES) * EDGES)
    sender = sender.reshape(EDGES // HID, HID)
    receiver = receiver.reshape(EDGES // HID, HID)
    edge_bias, edge_gain, node_bias, node_gain = (
        row.reshape(1, HID) for row in (edge_bias, edge_gain, node_bias, node_gain)
    )
    first, mid, second = make_packets(node_feat, send_rows)
    first, second = trade(first, second, GX)
    before = edge_before(
        node_feat,
        edge_feat,
        sender,
        receiver,
        edge_in_weight,
        edge_bias,
        edge_out_weight,
        node_in_weight,
        node_bias,
        node_out_weight,
    )
    second, first, before = join((second, first, before))
    first, mid, second = regroup((first, mid, second), 3 * SLOT)
    first, second = trade(first, second, GY)
    first, mid, second = regroup((first, mid, second), SLOT)
    first, second = trade(first, second, GZ)
    second, first = join((second, first))
    halo = (first, mid, second)
    rest = (receiver, node_feat, node_cot, edge_cot, edge_feat, edge_gain, node_gain)
    *back, own, got, base, edge_grad, square, rows = main_step(block_count, (*halo, *before, *rest))
    keep, give = weight_step(node_feat, *halo, *back, own, got, square, rows)
    taken = lax.ppermute(give, "c", SWAP)
    part = call(add_kernel, [(CELLS, HID)], [keep, taken])[0]
    part = scatter_half(part)
    second = lax.ppermute(back[2], GZ, swaps(GZ)[1])
    first, mid, second = regroup((taken, back[1], second), SLOT, 10**10)
    part, _ = join((part, mid))
    part = every_term(part)
    first, second = trade(first, second, GY)
    first, mid, second = regroup((first, mid, second), 3 * SLOT, 0)
    part, _ = join((part, mid))
    part = gather_half(part)
    first, second = trade(first, second, GX)
    second, first = join((second, first))
    node_grad = node_after(
        send_rows, first, mid, second, base, own, got, edge_in_weight
    )
    part, node_grad = join((part, node_grad))
    other = lax.ppermute(part, "c", SWAP)
    ein, eout, nin, nout, eb, eg, nb, ng = finish(part, other, scale)
    vectors = [row.reshape(HID) for row in (eb, eg, nb, ng)]
    return (
        node_grad,
        edge_grad,
        ein,
        vectors[0],
        eout,
        vectors[1],
        nin,
        vectors[2],
        nout,
        vectors[3],
    )


def solution(mesh):
    fine = jax.sharding.Mesh(mesh.devices.reshape(SPLIT), AXES)
    return jax.shard_map(
        on_device,
        mesh=fine,
        in_specs=(
            P(AXES, None),
            P(AXES, None),
            P(AXES, None),
            P(AXES, None),
            P(AXES),
            P(AXES),
            P(AXES),
            P(GX, GY, GZ, None),
            P(),
            P(),
            P(),
            P(),
            P(),
            P(),
            P(),
            P(),
        ),
        out_specs=(
            P(AXES, None),
            P(AXES, None),
            P(),
            P(),
            P(),
            P(),
            P(),
            P(),
            P(),
            P(),
        ),
        check_vma=False,
    )
```
